512 devices in a mesh: dp: 64 (over y, z), mp: 8 (over x, core).
Axes of the slice: x: 4, y: 8, z: 8, core: 2. Of those that a mesh axis runs over, the one named last changes fastest.
Arguments:
- activations: bfloat16 [8192, 5120], P('dp'), may hold values from -6 to 6
- cotangent: bfloat16 [8192, 17408], P('dp', 'mp'), may hold values from -6 to 6
- error_sketch: float32 [8, 2, 8, 16384], P('mp', None, None, 'dp'), may hold values from -24 to 24
- buckets: int32 [2, 40, 136], P(None, None, 'mp'), may hold values from 0 to 7
- sign_bits: int32 [2, 40, 136], P(None, None, 'mp'), may hold values from 0 to 1
- heavy_blocks: int32 [64], P('mp'), may hold values from 0 to 679
Outputs:
- update: float32 [8, 8, 16384], P('mp', None, 'dp')
- new_error: float32 [8, 2, 8, 16384], P('mp', None, None, 'dp')
The draws below stay inside these ranges and needn't reach their ends.
Inputs may be any that keep to these rules, and one draw needn't show every extreme that they name: `heavy_blocks`: block numbers are local to a hidden-unit shard: row block times 17408 / 1024 plus column block; repeats may occur.
All inputs are finite; a program needn't handle non-finite values.
Results may differ from the reference program's by a relative error of at most 0.0003.
Values sent between devices are 32-bit elements; how exact they have to be, the bound alone decides.
No kernel may reach another device: no remote copies, remote signals or barrier semaphores. Data moves between devices by JAX's collectives and lax.ppermute only.
A program may use at most 64 MiB of HBM per device.

```python
import jax
import jax.numpy as jnp
from jax import lax

D = 5120
FF = 17408
TOK_DEV = 128
BLK = 128
ROWS = 2
BUCKETS = 8
HEAVY = 8
CELLS = 16384
SHARD_BLOCKS = 680
TOKENS = 8192
N_MP = 8


def place_ends(entries, rng, smallest, high):
    index_at = [jax.random.randint(jax.random.fold_in(rng, axis), (), 0, length) for axis, length in enumerate(entries.shape)]
    main_axis = entries.shape.index(max(entries.shape))
    beside = index_at[:main_axis] + [(index_at[main_axis] + 1) % entries.shape[main_axis]] + index_at[main_axis + 1:]
    return entries.at[tuple(index_at)].set(smallest).at[tuple(beside)].set(high)


def shard_levels(stream_key, dims, split, low, high):
    level = 1.0
    for position, shards_of in split:
        draws = jax.random.uniform(jax.random.fold_in(jax.random.fold_in(stream_key, 6), position), (shards_of,), jnp.float32, low / len(split), high / len(split))
        level = level * jnp.repeat(jnp.exp(draws), dims[position] // shards_of).reshape((-1,) + (1,) * (len(dims) - 1 - position))
    return level


def gaussian(own_key, extent, scale, limit, pieces=(), kind=jnp.bfloat16):
    values = scale * jax.random.normal(own_key, extent, jnp.float32)
    if pieces:
        values = values * shard_levels(own_key, extent, pieces, -0.22, 0.18)
    return jnp.clip(values, -limit, limit).astype(kind)


def setup_inputs(seed: int = 0) -> dict:
    splits = jax.random.split(jax.random.key(seed), 7)
    activations = gaussian(splits[0], (TOKENS, D), 1.0, 6.0, ((0, 64),))
    cotangent = gaussian(splits[1], (TOKENS, FF), 1.0, 6.0, ((0, 64), (1, 8)))
    error_sketch = gaussian(splits[2], (N_MP, ROWS, BUCKETS, CELLS), 4.0, 24.0, ((0, 8), (3, 64)), jnp.float32)
    buckets = place_ends(jax.random.randint(splits[3], (ROWS, D // BLK, FF // BLK), 0, BUCKETS), jax.random.fold_in(splits[3], 1), 0, BUCKETS - 1).astype(jnp.int32)
    sign_bits = place_ends(jax.random.randint(splits[4], (ROWS, D // BLK, FF // BLK), 0, 2), jax.random.fold_in(splits[4], 1), 0, 1).astype(jnp.int32)
    heavy_blocks = place_ends(jax.random.randint(splits[5], (N_MP * HEAVY,), 0, SHARD_BLOCKS), jax.random.fold_in(splits[5], 1), 0, SHARD_BLOCKS - 1).astype(jnp.int32)
    return {"activations": activations, "cotangent": cotangent, "error_sketch": error_sketch, "buckets": buckets, "sign_bits": sign_bits, "heavy_blocks": heavy_blocks}


def reference(activations, cotangent, error_sketch, buckets, sign_bits, heavy_blocks):
    high = lax.Precision.HIGHEST
    act_full = activations.astype(jnp.float32)
    width = FF // N_MP
    col_blocks = width // BLK
    row_blocks = D // BLK
    count = row_blocks * col_blocks
    bucket_ids = jnp.arange(BUCKETS, dtype=jnp.int32)

    def shard(shard_id):
        cot_part = lax.dynamic_slice_in_dim(cotangent, shard_id * width, width, 1).astype(jnp.float32)
        gradient = jnp.dot(act_full.T, cot_part, precision=high) * (1.0 / TOK_DEV)
        blocks = gradient.reshape(row_blocks, BLK, col_blocks, BLK).transpose(0, 2, 1, 3).reshape(count, BLK * BLK)
        bucket_part = lax.dynamic_slice_in_dim(buckets, shard_id * col_blocks, col_blocks, 2).reshape(ROWS, count)
        sign_part = (2 * lax.dynamic_slice_in_dim(sign_bits, shard_id * col_blocks, col_blocks, 2) - 1).reshape(ROWS, count).astype(jnp.float32)
        sketch_map = (bucket_part[:, None, :] == bucket_ids[None, :, None]).astype(jnp.float32) * sign_part[:, None, :]
        sketch = jnp.einsum('rbn,ne->rbe', sketch_map, blocks, precision=high)
        heavy_ids = lax.dynamic_slice_in_dim(heavy_blocks, shard_id * HEAVY, HEAVY)
        exact = jnp.take(blocks, heavy_ids, axis=0)
        heavy_bucket = jnp.take(bucket_part, heavy_ids, axis=1)
        heavy_sign = jnp.take(sign_part, heavy_ids, axis=1)
        picks = (heavy_bucket[:, :, None] == bucket_ids[None, None, :]).astype(jnp.float32) * heavy_sign[:, :, None]
        error_part = error_sketch[shard_id]
        estimate = jnp.einsum('rkb,rbe->ke', picks, error_part, precision=high) * (1.0 / ROWS)
        update = estimate + exact
        new_error = error_part + sketch - jnp.einsum('rkb,ke->rbe', picks, update, precision=high)
        return update, new_error

    update, new_error = lax.map(shard, jnp.arange(N_MP, dtype=jnp.int32))
    return update, new_error
```

```python
import functools
import jax
import jax.numpy as jnp
from jax import lax
from jax.experimental import pallas as pl
from jax.experimental.pallas import tpu as pltpu
from jax.sharding import PartitionSpec as P

ROWS = 2
BUCKETS = 8
HEAVY = 8
BLK = 128
TOK = 128
ROW_BLOCKS = 40
COL_BLOCKS = 17
CPAD = 18
GRP = 4
GROUPS = TOK // GRP
KIN = GRP * ROW_BLOCKS
KC = GRP * CPAD
SKETCH = ROWS * BUCKETS
OUT_ROWS = HEAVY + SKETCH
DEPTH = GROUPS * KC
TN = (((0,), (0,)), ((), ()))
F32 = jnp.float32
BF16 = jnp.bfloat16
RBG = 4
UNROLL = 2
SIDE = 8
NEAR = [[(2 * a + i) * SIDE + 2 * b + j for i in range(2) for j in range(2)] for a in range(4) for b in range(4)]
FAR = [[(2 * a + i) * SIDE + 2 * b + j for a in range(4) for b in range(4)] for i in range(2) for j in range(2)]


def iota(shape, dim):
    return lax.broadcasted_iota(jnp.int32, shape, dim)


def place(p):
    dp = p // 2
    y, z = dp // SIDE, dp % SIDE
    return (((y % 2) * 2 + z % 2) * 16 + (y // 2) * 4 + z // 2) * 2 + p % 2


def kernel(act, cot, bkt, sgn, err, heavy, bkt_s, sgn_s, where, out, act3, cot3, maps, hi, lo, pick):
    perm = (place(iota((BLK, BLK), 0)) == iota((BLK, BLK), 1)).astype(BF16)
    for a in range(ROW_BLOCKS):
        act3[pl.ds(a, TOK, stride=ROW_BLOCKS), :] = jnp.dot(
            act[:, a * BLK : (a + 1) * BLK], perm, preferred_element_type=F32
        )
    for c in range(COL_BLOCKS):
        cot3[pl.ds(c, TOK, stride=CPAD), :] = cot[:, c * BLK : (c + 1) * BLK].astype(F32)
    cot3[pl.ds(COL_BLOCKS, TOK, stride=CPAD), :] = jnp.zeros((TOK, BLK), F32)

    spread_rows = (iota((KC, COL_BLOCKS), 0) % CPAD == iota((KC, COL_BLOCKS), 1)).astype(F32)
    spread_cols = (iota((ROW_BLOCKS, KIN), 1) % ROW_BLOCKS == iota((ROW_BLOCKS, KIN), 0)).astype(F32)
    own = (iota((KC, KIN), 0) // CPAD == iota((KC, KIN), 1) // ROW_BLOCKS) & (
        iota((KC, KIN), 0) % CPAD < COL_BLOCKS
    )
    for r in range(ROWS):
        codes = (bkt[:, r, :] + BUCKETS * sgn[:, r, :]).astype(F32)
        table = jnp.dot(
            jnp.dot(spread_rows, codes, preferred_element_type=F32), spread_cols, preferred_element_type=F32
        )
        table = jnp.where(own, table, -1.0)
        for b in range(0, BUCKETS, 2):
            two = []
            for bb in (b, b + 1):
                plus = (table == bb + BUCKETS).astype(F32)
                minus = (table == bb).astype(F32)
                two.append(plus - minus)
            at = (r * BUCKETS + b) * KC
            maps[at : at + 2 * KC, :] = jnp.concatenate(two, axis=0).astype(BF16)

    def weigh(i, carry):
        first = pl.multiple_of(i * 2 * KIN, 2 * KIN)
        rhs = jnp.concatenate(
            [act3[pl.ds(first, KIN), :], act3[pl.ds(first + KIN, KIN), :]], axis=1
        ).astype(BF16)
        rows = pl.ds(pl.multiple_of(i * 2 * KC, 2 * KC), 2 * KC)
        for g in range(0, SKETCH, RBG):
            many = jnp.dot(maps[g * KC : (g + RBG) * KC, :], rhs, preferred_element_type=F32)
            for j in range(RBG):
                w = many[j * KC : (j + 1) * KC]
                w = jnp.concatenate([w[:, :BLK], w[:, BLK:]], axis=0)
                top = w.astype(BF16)
                cols = slice((g + j) * BLK, (g + j + 1) * BLK)
                hi[rows, cols] = top
                lo[rows, cols] = (w - top.astype(F32)).astype(BF16)
        return carry

    lax.fori_loop(0, GROUPS // 2, weigh, 0, unroll=UNROLL)

    inverse = 1.0 / TOK
    for k in range(HEAVY):
        a = lax.div(heavy[k], COL_BLOCKS)
        c = lax.rem(heavy[k], COL_BLOCKS)
        block = lax.dot_general(
            act3[pl.ds(a, TOK, stride=ROW_BLOCKS), :].astype(BF16),
            cot[:, pl.ds(pl.multiple_of(c * BLK, BLK), BLK)],
            TN,
            preferred_element_type=F32,
        ) * inverse
        pick[k] = block
        out[pl.ds(k, BLK, stride=OUT_ROWS), :] = block

    lhs = cot3[...].T.astype(BF16)
    for rb in range(0, SKETCH, 2):
        cols = slice(rb * BLK, (rb + 2) * BLK)
        total = jnp.dot(lhs, hi[:, cols], preferred_element_type=F32) + jnp.dot(
            lhs, lo[:, cols], preferred_element_type=F32
        )
        for j in range(2):
            out[pl.ds(HEAVY + rb + j, BLK, stride=OUT_ROWS), :] = total[:, j * BLK : (j + 1) * BLK].T * inverse

    mine = place(2 * where[0]) * OUT_ROWS
    for k in range(HEAVY):
        a = lax.div(heavy[k], COL_BLOCKS)
        c = lax.rem(heavy[k], COL_BLOCKS)
        signs = [(2 * sgn_s[c, r, a] - 1).astype(F32) for r in range(ROWS)]
        rows = [r * BUCKETS + bkt_s[c, r, a] for r in range(ROWS)]
        for r in range(ROWS):
            at = pl.ds(HEAVY + rows[r], BLK, stride=OUT_ROWS)
            out[at, :] = out[at, :] - signs[r] * pick[k]
        for j in range(2):
            first = mine + j * OUT_ROWS
            guess = jnp.zeros((1, BLK), F32)
            for r in range(ROWS):
                guess = guess + signs[r] * err[pl.ds(j * SKETCH + rows[r], 1), :]
            guess = guess * (1.0 / ROWS)
            out[pl.ds(first + k, 1), :] = out[pl.ds(first + k, 1), :] + guess
            for r in range(ROWS):
                at = pl.ds(first + HEAVY + rows[r], 1)
                out[at, :] = out[at, :] - signs[r] * guess
    for j in range(2):
        at = pl.ds(mine + j * OUT_ROWS + HEAVY, SKETCH)
        out[at, :] = out[at, :] + err[j * SKETCH : (j + 1) * SKETCH, :]


def local_part(activations, cotangent, error_sketch, buckets, sign_bits, heavy_blocks, where):
    bkt, sgn = buckets.transpose(2, 0, 1), sign_bits.transpose(2, 0, 1)
    error = error_sketch.reshape(SKETCH, 2, BLK).transpose(1, 0, 2).reshape(2 * SKETCH, BLK)
    vmem = pl.BlockSpec(memory_space=pltpu.VMEM)
    smem = pl.BlockSpec(memory_space=pltpu.SMEM)
    return pl.pallas_call(
        kernel,
        out_shape=jax.ShapeDtypeStruct((BLK * OUT_ROWS, BLK), F32),
        in_specs=[vmem] * 5 + [smem] * 4,
        out_specs=vmem,
        scratch_shapes=[
            pltpu.VMEM((TOK * ROW_BLOCKS, BLK), F32),
            pltpu.VMEM((DEPTH, BLK), F32),
            pltpu.VMEM((SKETCH * KC, KIN), BF16),
            pltpu.VMEM((DEPTH, SKETCH * BLK), BF16),
            pltpu.VMEM((DEPTH, SKETCH * BLK), BF16),
            pltpu.VMEM((HEAVY, BLK, BLK), F32),
        ],
        compiler_params=pltpu.CompilerParams(vmem_limit_bytes=48 * 1024 * 1024),
        name="sketch_block",
    )(activations, cotangent, bkt, sgn, error, heavy_blocks, bkt, sgn, where)


def body(activations, cotangent, error_sketch, buckets, sign_bits, heavy_blocks):
    where = lax.axis_index("dp").astype(jnp.int32).reshape(1)
    local = local_part(activations, cotangent, error_sketch, buckets, sign_bits, heavy_blocks, where)
    part = lax.all_to_all(local.reshape(4, 32 * OUT_ROWS, BLK), "dp", 0, 0, axis_index_groups=NEAR).sum(axis=0)
    part = lax.all_to_all(part.reshape(16, 2 * OUT_ROWS, BLK), "dp", 0, 0, axis_index_groups=FAR).sum(axis=0)
    total = part.reshape(2, OUT_ROWS, BLK).transpose(1, 0, 2).reshape(3, 8, 2 * BLK)
    return total[:1], total[1:][None]


def solution(mesh):
    return jax.shard_map(
        body,
        mesh=mesh,
        in_specs=(
            P("dp", None),
            P("dp", "mp"),
            P("mp", None, None, "dp"),
            P(None, None, "mp"),
            P(None, None, "mp"),
            P("mp"),
        ),
        out_specs=(P("mp", None, "dp"), P("mp", None, None, "dp")),
        check_vma=False,
    )
```

```python
import functools
import jax
import jax.numpy as jnp
from jax import lax
from jax.experimental import pallas as pl
from jax.experimental.pallas import tpu as pltpu
from jax.sharding import PartitionSpec as P

ROWS = 2
BUCKETS = 8
HEAVY = 8
BLK = 128
TOK = 128
ROW_BLOCKS = 40
COL_BLOCKS = 17
CPAD = 18
GRP = 4
GROUPS = TOK // GRP
KIN = GRP * ROW_BLOCKS
KC = GRP * CPAD
SKETCH = ROWS * BUCKETS
OUT_ROWS = HEAVY + SKETCH
DEPTH = GROUPS * KC
TN = (((0,), (0,)), ((), ()))
F32 = jnp.float32
BF16 = jnp.bfloat16
PAIR = 4
BLOCKS = GROUPS // 2
CUTS = 1
SIDE = 8
NEAR = [[(2 * a + i) * SIDE + 2 * b + j for i in range(2) for j in range(2)] for a in range(4) for b in range(4)]
FAR = [[(2 * a + i) * SIDE + 2 * b + j for a in range(4) for b in range(4)] for i in range(2) for j in range(2)]


def iota(shape, dim):
    return lax.broadcasted_iota(jnp.int32, shape, dim)


def place(p):
    dp = p // 2
    y, z = dp // SIDE, dp % SIDE
    return (((y % 2) * 2 + z % 2) * 16 + (y // 2) * 4 + z // 2) * 2 + p % 2


def kernel(
    act_h, cot_h, err_h, bkt_h, sgn_h, heavy_h, where,
    out,
    act, cot, err4, bkt, sgn, heavy, bkt_s, sgn_s, err, act3, cot3, maps, actb, lhs, hi_a, lo_a, hi_b, lo_b, sems,
):
    pairs = [
        (bkt_h, bkt), (sgn_h, sgn), (act_h, act), (cot_h, cot),
        (heavy_h, heavy), (bkt_h, bkt_s), (sgn_h, sgn_s), (err_h, err4),
    ]
    copies = [pltpu.make_async_copy(a, b, sems.at[i]) for i, (a, b) in enumerate(pairs)]
    for copy in copies:
        copy.start()
    perm = (place(iota((BLK, BLK), 0)) == iota((BLK, BLK), 1)).astype(BF16)
    spread_rows = (iota((KC, COL_BLOCKS), 0) % CPAD == iota((KC, COL_BLOCKS), 1)).astype(F32)
    spread_cols = (iota((ROW_BLOCKS, KIN), 1) % ROW_BLOCKS == iota((ROW_BLOCKS, KIN), 0)).astype(F32)
    own = (iota((KC, KIN), 0) // CPAD == iota((KC, KIN), 1) // ROW_BLOCKS) & (
        iota((KC, KIN), 0) % CPAD < COL_BLOCKS
    )
    copies[0].wait()
    copies[1].wait()
    copies[4].wait()
    times = jnp.ones((COL_BLOCKS, ROW_BLOCKS), F32)
    for k in range(HEAVY):
        a, c = lax.div(heavy[k], COL_BLOCKS), lax.rem(heavy[k], COL_BLOCKS)
        here = (iota(times.shape, 0) == c) & (iota(times.shape, 1) == a)
        times = times - here.astype(F32)

    def spread(x):
        return jnp.dot(jnp.dot(spread_rows, x, preferred_element_type=F32), spread_cols, preferred_element_type=F32)

    for r in range(ROWS):
        weight = spread((2 * sgn[:, r, :] - 1).astype(F32) * times)
        bucket = jnp.where(own, spread(bkt[:, r, :].astype(F32)), -1.0)
        for b in range(0, BUCKETS, 2):
            two = [jnp.where(bucket == bb, weight, 0.0) for bb in (b, b + 1)]
            at = (r * BUCKETS + b) * KC
            maps[at : at + 2 * KC, :] = jnp.concatenate(two, axis=0).astype(BF16)

    copies[2].wait()
    for a in range(ROW_BLOCKS):
        act3[pl.ds(a, TOK, stride=ROW_BLOCKS), :] = jnp.dot(
            act[:, a * BLK : (a + 1) * BLK], perm, preferred_element_type=F32
        )
    copies[3].wait()
    for c in range(COL_BLOCKS):
        cot3[pl.ds(c, TOK, stride=CPAD), :] = cot[:, c * BLK : (c + 1) * BLK].astype(F32)
    cot3[pl.ds(COL_BLOCKS, TOK, stride=CPAD), :] = jnp.zeros((TOK, BLK), F32)

    inverse = 1.0 / TOK
    for copy in copies[5:]:
        copy.wait()
    for r in range(ROWS):
        for j in range(2):
            err[j * SKETCH + r * BUCKETS : j * SKETCH + (r + 1) * BUCKETS, :] = err4[0, r, :, j * BLK : (j + 1) * BLK]
    for k in range(HEAVY):
        a = lax.div(heavy[k], COL_BLOCKS)
        c = lax.rem(heavy[k], COL_BLOCKS)
        block = lax.dot_general(
            act3[pl.ds(a, TOK, stride=ROW_BLOCKS), :].astype(BF16),
            cot[:, pl.ds(pl.multiple_of(c * BLK, BLK), BLK)],
            TN,
            preferred_element_type=F32,
        ) * inverse
        out[pl.ds(k, BLK, stride=OUT_ROWS), :] = block

    for i in range(BLOCKS):
        for h in range(2):
            actb[i, :, h * BLK : (h + 1) * BLK] = act3[(2 * i + h) * KIN : (2 * i + h + 1) * KIN, :].astype(BF16)
    lhs[...] = cot3[...].T.astype(BF16)

    def weigh(g, i, hi, lo):
        many = jnp.dot(maps[g * PAIR * KC : (g + 1) * PAIR * KC, :], actb[i], preferred_element_type=F32)
        rows = slice(i * 2 * KC, (i + 1) * 2 * KC)
        for j in range(PAIR):
            w = many[j * KC : (j + 1) * KC]
            w = jnp.concatenate([w[:, :BLK], w[:, BLK:]], axis=0)
            top = w.astype(BF16)
            hi[rows, j * BLK : (j + 1) * BLK] = top
            lo[rows, j * BLK : (j + 1) * BLK] = (w - top.astype(F32)).astype(BF16)

    def fold(g, hi, lo):
        for t in range(PAIR // 2):
            total = None
            for part in (hi, lo):
                for k in range(CUTS):
                    deep = slice(k * DEPTH // CUTS, (k + 1) * DEPTH // CUTS)
                    term = jnp.dot(
                        lhs[:, deep], part[deep, 2 * t * BLK : 2 * (t + 1) * BLK], preferred_element_type=F32
                    )
                    total = term if total is None else total + term
                    yield
            for j in range(2):
                at = HEAVY + g * PAIR + 2 * t + j
                out[pl.ds(at, BLK, stride=OUT_ROWS), :] = total[:, j * BLK : (j + 1) * BLK].T * inverse

    steps = SKETCH // PAIR
    slots = [(hi_a, lo_a), (hi_b, lo_b)]
    for i in range(BLOCKS):
        weigh(0, i, *slots[0])
    for g in range(steps):
        sums = fold(g, *slots[g % 2])
        count = PAIR * CUTS
        done = 0
        for i in range(BLOCKS):
            if g + 1 < steps:
                weigh(g + 1, i, *slots[(g + 1) % 2])
            while done * BLOCKS < (i + 1) * count:
                next(sums, None)
                done += 1
        for _ in sums:
            pass

    mine = place(2 * where[0]) * OUT_ROWS
    for k in range(HEAVY):
        a = lax.div(heavy[k], COL_BLOCKS)
        c = lax.rem(heavy[k], COL_BLOCKS)
        signs = [(2 * sgn_s[c, r, a] - 1).astype(F32) for r in range(ROWS)]
        rows = [r * BUCKETS + bkt_s[c, r, a] for r in range(ROWS)]
        for j in range(2):
            first = mine + j * OUT_ROWS
            guess = jnp.zeros((1, BLK), F32)
            for r in range(ROWS):
                guess = guess + signs[r] * err[pl.ds(j * SKETCH + rows[r], 1), :]
            guess = guess * (1.0 / ROWS)
            out[pl.ds(first + k, 1), :] = out[pl.ds(first + k, 1), :] + guess
            for r in range(ROWS):
                at = pl.ds(first + HEAVY + rows[r], 1)
                out[at, :] = out[at, :] - signs[r] * guess
    for j in range(2):
        at = pl.ds(mine + j * OUT_ROWS + HEAVY, SKETCH)
        out[at, :] = out[at, :] + err[j * SKETCH : (j + 1) * SKETCH, :]


def local_part(activations, cotangent, error_sketch, buckets, sign_bits, heavy_blocks, where):
    bkt, sgn = buckets.transpose(2, 0, 1), sign_bits.transpose(2, 0, 1)
    hbm = pl.BlockSpec(memory_space=pltpu.HBM)
    return pl.pallas_call(
        kernel,
        out_shape=jax.ShapeDtypeStruct((BLK * OUT_ROWS, BLK), F32),
        in_specs=[hbm] * 6 + [pl.BlockSpec(memory_space=pltpu.SMEM)],
        out_specs=pl.BlockSpec(memory_space=pltpu.VMEM),
        scratch_shapes=[
            pltpu.VMEM(activations.shape, BF16),
            pltpu.VMEM(cotangent.shape, BF16),
            pltpu.VMEM(error_sketch.shape, F32),
            pltpu.VMEM(bkt.shape, jnp.int32),
            pltpu.VMEM(sgn.shape, jnp.int32),
            pltpu.SMEM(heavy_blocks.shape, jnp.int32),
            pltpu.SMEM(bkt.shape, jnp.int32),
            pltpu.SMEM(sgn.shape, jnp.int32),
            pltpu.VMEM((2 * SKETCH, BLK), F32),
            pltpu.VMEM((TOK * ROW_BLOCKS, BLK), F32),
            pltpu.VMEM((DEPTH, BLK), F32),
            pltpu.VMEM((SKETCH * KC, KIN), BF16),
            pltpu.VMEM((BLOCKS, KIN, 2 * BLK), BF16),
            pltpu.VMEM((BLK, DEPTH), BF16),
            pltpu.VMEM((DEPTH, PAIR * BLK), BF16),
            pltpu.VMEM((DEPTH, PAIR * BLK), BF16),
            pltpu.VMEM((DEPTH, PAIR * BLK), BF16),
            pltpu.VMEM((DEPTH, PAIR * BLK), BF16),
            pltpu.SemaphoreType.DMA((8,)),
        ],
        compiler_params=pltpu.CompilerParams(vmem_limit_bytes=60 * 1024 * 1024),
        name="sketch_block",
    )(activations, cotangent, error_sketch, bkt, sgn, heavy_blocks, where)


def body(activations, cotangent, error_sketch, buckets, sign_bits, heavy_blocks):
    where = lax.axis_index("dp").astype(jnp.int32).reshape(1)
    local = local_part(activations, cotangent, error_sketch, buckets, sign_bits, heavy_blocks, where)
    part = lax.all_to_all(local.reshape(4, 32 * OUT_ROWS, BLK), "dp", 0, 0, axis_index_groups=NEAR).sum(axis=0)
    part = lax.all_to_all(part.reshape(16, 2 * OUT_ROWS, BLK), "dp", 0, 0, axis_index_groups=FAR).sum(axis=0)
    total = part.reshape(2, OUT_ROWS, BLK).transpose(1, 0, 2).reshape(3, 8, 2 * BLK)
    return total[:1], total[1:][None]


def solution(mesh):
    return jax.shard_map(
        body,
        mesh=mesh,
        in_specs=(
            P("dp", None),
            P("dp", "mp"),
            P("mp", None, None, "dp"),
            P(None, None, "mp"),
            P(None, None, "mp"),
            P("mp"),
        ),
        out_specs=(P("mp", None, "dp"), P("mp", None, None, "dp")),
        check_vma=False,
    )
```

```python
import functools
import jax
import jax.numpy as jnp
from jax import lax
from jax.experimental import pallas as pl
from jax.experimental.pallas import tpu as pltpu
from jax.sharding import PartitionSpec as P

ROWS = 2
BUCKETS = 8
HEAVY = 8
BLK = 128
TOK = 128
ROW_BLOCKS = 40
COL_BLOCKS = 17
CPAD = 18
GRP = 4
GROUPS = TOK // GRP
KIN = GRP * ROW_BLOCKS
KC = GRP * CPAD
SKETCH = ROWS * BUCKETS
OUT_ROWS = HEAVY + SKETCH
DEPTH = GROUPS * KC
TN = (((0,), (0,)), ((), ()))
F32 = jnp.float32
BF16 = jnp.bfloat16
PAIR = 4
BLOCKS = GROUPS // 2
CUTS = 1
SIDE = 8
MODEL = 8


def mate(v, half):
    return (v + 1 if (v + half) % 2 == 0 else v - 1) % SIDE


def near_groups():
    groups = set()
    for m in range(MODEL):
        for y in range(SIDE):
            for z in range(SIDE):
                ys, zs = {y, mate(y, m % 2)}, {z, mate(z, m % 2)}
                groups.add(
                    tuple(
                        (u * SIDE + v) * MODEL + m
                        for u in sorted(ys, key=lambda t: t % 2)
                        for v in sorted(zs, key=lambda t: t % 2)
                    )
                )
    return [list(g) for g in sorted(groups)]


NEAR = near_groups()
FAR = [[(2 * a + i) * SIDE + 2 * b + j for a in range(4) for b in range(4)] for i in range(2) for j in range(2)]


def iota(shape, dim):
    return lax.broadcasted_iota(jnp.int32, shape, dim)


def place(p):
    dp = p // 2
    y, z = dp // SIDE, dp % SIDE
    return (((y % 2) * 2 + z % 2) * 16 + (y // 2) * 4 + z // 2) * 2 + p % 2


def kernel(
    act_h, cot_h, err_h, bkt_h, sgn_h, heavy_h, where,
    out,
    act, cot, err4, bkt, sgn, heavy, bkt_s, sgn_s, err, act3, cot3, maps, actb, lhs, hi_a, lo_a, hi_b, lo_b, sems,
):
    pairs = [
        (bkt_h, bkt), (sgn_h, sgn), (act_h, act), (cot_h, cot),
        (heavy_h, heavy), (bkt_h, bkt_s), (sgn_h, sgn_s), (err_h, err4),
    ]
    copies = [pltpu.make_async_copy(a, b, sems.at[i]) for i, (a, b) in enumerate(pairs)]
    for copy in copies:
        copy.start()
    perm = (place(iota((BLK, BLK), 0)) == iota((BLK, BLK), 1)).astype(BF16)
    spread_rows = (iota((KC, COL_BLOCKS), 0) % CPAD == iota((KC, COL_BLOCKS), 1)).astype(F32)
    spread_cols = (iota((ROW_BLOCKS, KIN), 1) % ROW_BLOCKS == iota((ROW_BLOCKS, KIN), 0)).astype(F32)
    own = (iota((KC, KIN), 0) // CPAD == iota((KC, KIN), 1) // ROW_BLOCKS) & (
        iota((KC, KIN), 0) % CPAD < COL_BLOCKS
    )
    copies[0].wait()
    copies[1].wait()
    copies[4].wait()
    times = jnp.ones((COL_BLOCKS, ROW_BLOCKS), F32)
    for k in range(HEAVY):
        a, c = lax.div(heavy[k], COL_BLOCKS), lax.rem(heavy[k], COL_BLOCKS)
        here = (iota(times.shape, 0) == c) & (iota(times.shape, 1) == a)
        times = times - here.astype(F32)

    def spread(x):
        return jnp.dot(jnp.dot(spread_rows, x, preferred_element_type=F32), spread_cols, preferred_element_type=F32)

    for r in range(ROWS):
        weight = spread((2 * sgn[:, r, :] - 1).astype(F32) * times)
        bucket = jnp.where(own, spread(bkt[:, r, :].astype(F32)), -1.0)
        for b in range(0, BUCKETS, 2):
            two = [jnp.where(bucket == bb, weight, 0.0) for bb in (b, b + 1)]
            at = (r * BUCKETS + b) * KC
            maps[at : at + 2 * KC, :] = jnp.concatenate(two, axis=0).astype(BF16)

    copies[2].wait()
    for a in range(ROW_BLOCKS):
        act3[pl.ds(a, TOK, stride=ROW_BLOCKS), :] = jnp.dot(
            act[:, a * BLK : (a + 1) * BLK], perm, preferred_element_type=F32
        )
    copies[3].wait()
    for c in range(COL_BLOCKS):
        cot3[pl.ds(c, TOK, stride=CPAD), :] = cot[:, c * BLK : (c + 1) * BLK].astype(F32)
    cot3[pl.ds(COL_BLOCKS, TOK, stride=CPAD), :] = jnp.zeros((TOK, BLK), F32)

    inverse = 1.0 / TOK
    for copy in copies[5:]:
        copy.wait()
    for r in range(ROWS):
        for j in range(2):
            err[j * SKETCH + r * BUCKETS : j * SKETCH + (r + 1) * BUCKETS, :] = err4[0, r, :, j * BLK : (j + 1) * BLK]
    for k in range(HEAVY):
        a = lax.div(heavy[k], COL_BLOCKS)
        c = lax.rem(heavy[k], COL_BLOCKS)
        block = lax.dot_general(
            act3[pl.ds(a, TOK, stride=ROW_BLOCKS), :].astype(BF16),
            cot[:, pl.ds(pl.multiple_of(c * BLK, BLK), BLK)],
            TN,
            preferred_element_type=F32,
        ) * inverse
        out[pl.ds(k, BLK, stride=OUT_ROWS), :] = block

    for i in range(BLOCKS):
        for h in range(2):
            actb[i, :, h * BLK : (h + 1) * BLK] = act3[(2 * i + h) * KIN : (2 * i + h + 1) * KIN, :].astype(BF16)
    lhs[...] = cot3[...].T.astype(BF16)

    def weigh(g, i, hi, lo):
        many = jnp.dot(maps[g * PAIR * KC : (g + 1) * PAIR * KC, :], actb[i], preferred_element_type=F32)
        rows = slice(i * 2 * KC, (i + 1) * 2 * KC)
        for j in range(PAIR):
            w = many[j * KC : (j + 1) * KC]
            w = jnp.concatenate([w[:, :BLK], w[:, BLK:]], axis=0)
            top = w.astype(BF16)
            hi[rows, j * BLK : (j + 1) * BLK] = top
            lo[rows, j * BLK : (j + 1) * BLK] = (w - top.astype(F32)).astype(BF16)

    def fold(g, hi, lo):
        for t in range(PAIR // 2):
            total = None
            for part in (hi, lo):
                for k in range(CUTS):
                    deep = slice(k * DEPTH // CUTS, (k + 1) * DEPTH // CUTS)
                    term = jnp.dot(
                        lhs[:, deep], part[deep, 2 * t * BLK : 2 * (t + 1) * BLK], preferred_element_type=F32
                    )
                    total = term if total is None else total + term
                    yield
            for j in range(2):
                at = HEAVY + g * PAIR + 2 * t + j
                out[pl.ds(at, BLK, stride=OUT_ROWS), :] = total[:, j * BLK : (j + 1) * BLK].T * inverse

    steps = SKETCH // PAIR
    slots = [(hi_a, lo_a), (hi_b, lo_b)]
    for i in range(BLOCKS):
        weigh(0, i, *slots[0])
    for g in range(steps):
        sums = fold(g, *slots[g % 2])
        count = PAIR * CUTS
        done = 0
        for i in range(BLOCKS):
            if g + 1 < steps:
                weigh(g + 1, i, *slots[(g + 1) % 2])
            while done * BLOCKS < (i + 1) * count:
                next(sums, None)
                done += 1
        for _ in sums:
            pass

    mine = place(2 * where[0]) * OUT_ROWS
    for k in range(HEAVY):
        a = lax.div(heavy[k], COL_BLOCKS)
        c = lax.rem(heavy[k], COL_BLOCKS)
        signs = [(2 * sgn_s[c, r, a] - 1).astype(F32) for r in range(ROWS)]
        rows = [r * BUCKETS + bkt_s[c, r, a] for r in range(ROWS)]
        for j in range(2):
            first = mine + j * OUT_ROWS
            guess = jnp.zeros((1, BLK), F32)
            for r in range(ROWS):
                guess = guess + signs[r] * err[pl.ds(j * SKETCH + rows[r], 1), :]
            guess = guess * (1.0 / ROWS)
            out[pl.ds(first + k, 1), :] = out[pl.ds(first + k, 1), :] + guess
            for r in range(ROWS):
                at = pl.ds(first + HEAVY + rows[r], 1)
                out[at, :] = out[at, :] - signs[r] * guess
    for j in range(2):
        at = pl.ds(mine + j * OUT_ROWS + HEAVY, SKETCH)
        out[at, :] = out[at, :] + err[j * SKETCH : (j + 1) * SKETCH, :]


def local_part(activations, cotangent, error_sketch, buckets, sign_bits, heavy_blocks, where):
    bkt, sgn = buckets.transpose(2, 0, 1), sign_bits.transpose(2, 0, 1)
    hbm = pl.BlockSpec(memory_space=pltpu.HBM)
    return pl.pallas_call(
        kernel,
        out_shape=jax.ShapeDtypeStruct((BLK * OUT_ROWS, BLK), F32),
        in_specs=[hbm] * 6 + [pl.BlockSpec(memory_space=pltpu.SMEM)],
        out_specs=pl.BlockSpec(memory_space=pltpu.VMEM),
        scratch_shapes=[
            pltpu.VMEM(activations.shape, BF16),
            pltpu.VMEM(cotangent.shape, BF16),
            pltpu.VMEM(error_sketch.shape, F32),
            pltpu.VMEM(bkt.shape, jnp.int32),
            pltpu.VMEM(sgn.shape, jnp.int32),
            pltpu.SMEM(heavy_blocks.shape, jnp.int32),
            pltpu.SMEM(bkt.shape, jnp.int32),
            pltpu.SMEM(sgn.shape, jnp.int32),
            pltpu.VMEM((2 * SKETCH, BLK), F32),
            pltpu.VMEM((TOK * ROW_BLOCKS, BLK), F32),
            pltpu.VMEM((DEPTH, BLK), F32),
            pltpu.VMEM((SKETCH * KC, KIN), BF16),
            pltpu.VMEM((BLOCKS, KIN, 2 * BLK), BF16),
            pltpu.VMEM((BLK, DEPTH), BF16),
            pltpu.VMEM((DEPTH, PAIR * BLK), BF16),
            pltpu.VMEM((DEPTH, PAIR * BLK), BF16),
            pltpu.VMEM((DEPTH, PAIR * BLK), BF16),
            pltpu.VMEM((DEPTH, PAIR * BLK), BF16),
            pltpu.SemaphoreType.DMA((8,)),
        ],
        compiler_params=pltpu.CompilerParams(vmem_limit_bytes=60 * 1024 * 1024),
        name="sketch_block",
    )(activations, cotangent, error_sketch, bkt, sgn, heavy_blocks, where)


def body(activations, cotangent, error_sketch, buckets, sign_bits, heavy_blocks):
    where = lax.axis_index("dp").astype(jnp.int32).reshape(1)
    local = local_part(activations, cotangent, error_sketch, buckets, sign_bits, heavy_blocks, where)
    part = lax.all_to_all(local.reshape(4, 32 * OUT_ROWS, BLK), ("dp", "mp"), 0, 0, axis_index_groups=NEAR).sum(axis=0)
    part = lax.all_to_all(part.reshape(16, 2 * OUT_ROWS, BLK), "dp", 0, 0, axis_index_groups=FAR).sum(axis=0)
    total = part.reshape(2, OUT_ROWS, BLK).transpose(1, 0, 2).reshape(3, 8, 2 * BLK)
    return total[:1], total[1:][None]


def solution(mesh):
    return jax.shard_map(
        body,
        mesh=mesh,
        in_specs=(
            P("dp", None),
            P("dp", "mp"),
            P("mp", None, None, "dp"),
            P(None, None, "mp"),
            P(None, None, "mp"),
            P("mp"),
        ),
        out_specs=(P("mp", None, "dp"), P("mp", None, None, "dp")),
        check_vma=False,
    )
```

```python
import functools
import jax
import jax.numpy as jnp
from jax import lax
from jax.experimental import pallas as pl
from jax.experimental.pallas import tpu as pltpu
from jax.sharding import PartitionSpec as P

ROWS = 2
BUCKETS = 8
HEAVY = 8
BLK = 128
TOK = 128
ROW_BLOCKS = 40
COL_BLOCKS = 17
CPAD = 18
GRP = 4
GROUPS = TOK // GRP
KIN = GRP * ROW_BLOCKS
KC = GRP * CPAD
SKETCH = ROWS * BUCKETS
OUT_ROWS = HEAVY + SKETCH
DEPTH = GROUPS * KC
TN = (((0,), (0,)), ((), ()))
F32 = jnp.float32
BF16 = jnp.bfloat16
PAIR = 4
BLOCKS = GROUPS // 2
CUTS = 1
SIDE = 8
MODEL = 8


def mate(v, half):
    return (v + 1 if (v + half) % 2 == 0 else v - 1) % SIDE


def near_pairs(step):
    pairs = []
    for y in range(SIDE):
        for z in range(SIDE):
            for m in range(MODEL):
                u = mate(y, m % 2) if step & 2 else y
                v = mate(z, m % 2) if step & 1 else z
                pairs.append(((y * SIDE + z) * MODEL + m, (u * SIDE + v) * MODEL + m))
    return pairs


FAR = [[(2 * a + i) * SIDE + 2 * b + j for a in range(4) for b in range(4)] for i in range(2) for j in range(2)]


def iota(shape, dim):
    return lax.broadcasted_iota(jnp.int32, shape, dim)


def place(p):
    dp = p // 2
    y, z = dp // SIDE, dp % SIDE
    return (((y % 2) * 2 + z % 2) * 16 + (y // 2) * 4 + z // 2) * 2 + p % 2


def kernel(
    act_h, cot_h, err_h, bkt_h, sgn_h, heavy_h, where,
    out_0, out_1, out_2, out_3,
    act, cot, err4, bkt, sgn, heavy, bkt_s, sgn_s, err, act3, cot3, maps, actb, lhs, hi_a, lo_a, hi_b, lo_b, out, sems, out_sems,
):
    pairs = [
        (bkt_h, bkt), (sgn_h, sgn), (act_h, act), (cot_h, cot),
        (heavy_h, heavy), (bkt_h, bkt_s), (sgn_h, sgn_s), (err_h, err4),
    ]
    copies = [pltpu.make_async_copy(a, b, sems.at[i]) for i, (a, b) in enumerate(pairs)]
    for copy in copies:
        copy.start()
    perm = (place(iota((BLK, BLK), 0)) == iota((BLK, BLK), 1)).astype(BF16)
    spread_rows = (iota((KC, COL_BLOCKS), 0) % CPAD == iota((KC, COL_BLOCKS), 1)).astype(F32)
    spread_cols = (iota((ROW_BLOCKS, KIN), 1) % ROW_BLOCKS == iota((ROW_BLOCKS, KIN), 0)).astype(F32)
    own = (iota((KC, KIN), 0) // CPAD == iota((KC, KIN), 1) // ROW_BLOCKS) & (
        iota((KC, KIN), 0) % CPAD < COL_BLOCKS
    )
    copies[0].wait()
    copies[1].wait()
    copies[4].wait()
    times = jnp.ones((COL_BLOCKS, ROW_BLOCKS), F32)
    for k in range(HEAVY):
        a, c = lax.div(heavy[k], COL_BLOCKS), lax.rem(heavy[k], COL_BLOCKS)
        here = (iota(times.shape, 0) == c) & (iota(times.shape, 1) == a)
        times = times - here.astype(F32)

    def spread(x):
        return jnp.dot(jnp.dot(spread_rows, x, preferred_element_type=F32), spread_cols, preferred_element_type=F32)

    for r in range(ROWS):
        weight = spread((2 * sgn[:, r, :] - 1).astype(F32) * times)
        bucket = jnp.where(own, spread(bkt[:, r, :].astype(F32)), -1.0)
        for b in range(0, BUCKETS, 2):
            two = [jnp.where(bucket == bb, weight, 0.0) for bb in (b, b + 1)]
            at = (r * BUCKETS + b) * KC
            maps[at : at + 2 * KC, :] = jnp.concatenate(two, axis=0).astype(BF16)

    copies[2].wait()
    for a in range(ROW_BLOCKS):
        act3[pl.ds(a, TOK, stride=ROW_BLOCKS), :] = jnp.dot(
            act[:, a * BLK : (a + 1) * BLK], perm, preferred_element_type=F32
        )
    copies[3].wait()
    for c in range(COL_BLOCKS):
        cot3[pl.ds(c, TOK, stride=CPAD), :] = cot[:, c * BLK : (c + 1) * BLK].astype(F32)
    cot3[pl.ds(COL_BLOCKS, TOK, stride=CPAD), :] = jnp.zeros((TOK, BLK), F32)

    inverse = 1.0 / TOK
    for copy in copies[5:]:
        copy.wait()
    for r in range(ROWS):
        for j in range(2):
            err[j * SKETCH + r * BUCKETS : j * SKETCH + (r + 1) * BUCKETS, :] = err4[0, r, :, j * BLK : (j + 1) * BLK]
    for k in range(HEAVY):
        a = lax.div(heavy[k], COL_BLOCKS)
        c = lax.rem(heavy[k], COL_BLOCKS)
        block = lax.dot_general(
            act3[pl.ds(a, TOK, stride=ROW_BLOCKS), :].astype(BF16),
            cot[:, pl.ds(pl.multiple_of(c * BLK, BLK), BLK)],
            TN,
            preferred_element_type=F32,
        ) * inverse
        out[pl.ds(k, BLK, stride=OUT_ROWS), :] = block

    for i in range(BLOCKS):
        for h in range(2):
            actb[i, :, h * BLK : (h + 1) * BLK] = act3[(2 * i + h) * KIN : (2 * i + h + 1) * KIN, :].astype(BF16)
    lhs[...] = cot3[...].T.astype(BF16)

    def weigh(g, i, hi, lo):
        many = jnp.dot(maps[g * PAIR * KC : (g + 1) * PAIR * KC, :], actb[i], preferred_element_type=F32)
        rows = slice(i * 2 * KC, (i + 1) * 2 * KC)
        for j in range(PAIR):
            w = many[j * KC : (j + 1) * KC]
            w = jnp.concatenate([w[:, :BLK], w[:, BLK:]], axis=0)
            top = w.astype(BF16)
            hi[rows, j * BLK : (j + 1) * BLK] = top
            lo[rows, j * BLK : (j + 1) * BLK] = (w - top.astype(F32)).astype(BF16)

    def fold(g, hi, lo):
        for t in range(PAIR // 2):
            total = None
            for part in (hi, lo):
                for k in range(CUTS):
                    deep = slice(k * DEPTH // CUTS, (k + 1) * DEPTH // CUTS)
                    term = jnp.dot(
                        lhs[:, deep], part[deep, 2 * t * BLK : 2 * (t + 1) * BLK], preferred_element_type=F32
                    )
                    total = term if total is None else total + term
                    yield
            for j in range(2):
                at = HEAVY + g * PAIR + 2 * t + j
                out[pl.ds(at, BLK, stride=OUT_ROWS), :] = total[:, j * BLK : (j + 1) * BLK].T * inverse

    steps = SKETCH // PAIR
    slots = [(hi_a, lo_a), (hi_b, lo_b)]
    for i in range(BLOCKS):
        weigh(0, i, *slots[0])
    for g in range(steps):
        sums = fold(g, *slots[g % 2])
        count = PAIR * CUTS
        done = 0
        for i in range(BLOCKS):
            if g + 1 < steps:
                weigh(g + 1, i, *slots[(g + 1) % 2])
            while done * BLOCKS < (i + 1) * count:
                next(sums, None)
                done += 1
        for _ in sums:
            pass

    mine = place(2 * where[0]) * OUT_ROWS
    for k in range(HEAVY):
        a = lax.div(heavy[k], COL_BLOCKS)
        c = lax.rem(heavy[k], COL_BLOCKS)
        signs = [(2 * sgn_s[c, r, a] - 1).astype(F32) for r in range(ROWS)]
        rows = [r * BUCKETS + bkt_s[c, r, a] for r in range(ROWS)]
        for j in range(2):
            first = mine + j * OUT_ROWS
            guess = jnp.zeros((1, BLK), F32)
            for r in range(ROWS):
                guess = guess + signs[r] * err[pl.ds(j * SKETCH + rows[r], 1), :]
            guess = guess * (1.0 / ROWS)
            out[pl.ds(first + k, 1), :] = out[pl.ds(first + k, 1), :] + guess
            for r in range(ROWS):
                at = pl.ds(first + HEAVY + rows[r], 1)
                out[at, :] = out[at, :] - signs[r] * guess
    for j in range(2):
        at = pl.ds(mine + j * OUT_ROWS + HEAVY, SKETCH)
        out[at, :] = out[at, :] + err[j * SKETCH : (j + 1) * SKETCH, :]

    quarter = BLK // 4 * OUT_ROWS
    own_class = (where[0] // SIDE % 2) * 2 + where[0] % 2
    sends = []
    for step, part in enumerate((out_0, out_1, out_2, out_3)):
        first = pl.multiple_of((own_class ^ step) * quarter, quarter)
        sends.append(pltpu.make_async_copy(out.at[pl.ds(first, quarter), :], part, out_sems.at[step]))
    for send in sends:
        send.start()
    for send in sends:
        send.wait()


def local_part(activations, cotangent, error_sketch, buckets, sign_bits, heavy_blocks, where):
    bkt, sgn = buckets.transpose(2, 0, 1), sign_bits.transpose(2, 0, 1)
    hbm = pl.BlockSpec(memory_space=pltpu.HBM)
    return pl.pallas_call(
        kernel,
        out_shape=[jax.ShapeDtypeStruct((BLK // 4 * OUT_ROWS, BLK), F32)] * 4,
        in_specs=[hbm] * 6 + [pl.BlockSpec(memory_space=pltpu.SMEM)],
        out_specs=[hbm] * 4,
        scratch_shapes=[
            pltpu.VMEM(activations.shape, BF16),
            pltpu.VMEM(cotangent.shape, BF16),
            pltpu.VMEM(error_sketch.shape, F32),
            pltpu.VMEM(bkt.shape, jnp.int32),
            pltpu.VMEM(sgn.shape, jnp.int32),
            pltpu.SMEM(heavy_blocks.shape, jnp.int32),
            pltpu.SMEM(bkt.shape, jnp.int32),
            pltpu.SMEM(sgn.shape, jnp.int32),
            pltpu.VMEM((2 * SKETCH, BLK), F32),
            pltpu.VMEM((TOK * ROW_BLOCKS, BLK), F32),
            pltpu.VMEM((DEPTH, BLK), F32),
            pltpu.VMEM((SKETCH * KC, KIN), BF16),
            pltpu.VMEM((BLOCKS, KIN, 2 * BLK), BF16),
            pltpu.VMEM((BLK, DEPTH), BF16),
            pltpu.VMEM((DEPTH, PAIR * BLK), BF16),
            pltpu.VMEM((DEPTH, PAIR * BLK), BF16),
            pltpu.VMEM((DEPTH, PAIR * BLK), BF16),
            pltpu.VMEM((DEPTH, PAIR * BLK), BF16),
            pltpu.VMEM((BLK * OUT_ROWS, BLK), F32),
            pltpu.SemaphoreType.DMA((8,)),
            pltpu.SemaphoreType.DMA((4,)),
        ],
        compiler_params=pltpu.CompilerParams(vmem_limit_bytes=60 * 1024 * 1024),
        name="sketch_block",
    )(activations, cotangent, error_sketch, bkt, sgn, heavy_blocks, where)


def finish(parts, update, new_error):
    total = jnp.sum(parts[...], axis=0)
    for j in range(2):
        cols = slice(j * BLK, (j + 1) * BLK)
        row = j * OUT_ROWS
        update[0, :, cols] = total[row : row + HEAVY]
        for r in range(ROWS):
            first = row + HEAVY + r * BUCKETS
            new_error[0, r, :, cols] = total[first : first + BUCKETS]


def outputs(parts):
    vmem = pl.BlockSpec(memory_space=pltpu.VMEM)
    return pl.pallas_call(
        finish,
        out_shape=(
            jax.ShapeDtypeStruct((1, HEAVY, 2 * BLK), F32),
            jax.ShapeDtypeStruct((1, ROWS, BUCKETS, 2 * BLK), F32),
        ),
        in_specs=[vmem],
        out_specs=(vmem, vmem),
        name="outputs",
    )(parts)


def body(activations, cotangent, error_sketch, buckets, sign_bits, heavy_blocks):
    where = lax.axis_index("dp").astype(jnp.int32).reshape(1)
    part, *others = local_part(activations, cotangent, error_sketch, buckets, sign_bits, heavy_blocks, where)
    for step in (3, 2, 1):
        part = part + lax.ppermute(others[step - 1], ("dp", "mp"), near_pairs(step))
    parts = lax.all_to_all(part.reshape(16, 2 * OUT_ROWS, BLK), "dp", 0, 0, axis_index_groups=FAR)
    return outputs(parts)


def solution(mesh):
    return jax.shard_map(
        body,
        mesh=mesh,
        in_specs=(
            P("dp", None),
            P("dp", "mp"),
            P("mp", None, None, "dp"),
            P(None, None, "mp"),
            P(None, None, "mp"),
            P("mp"),
        ),
        out_specs=(P("mp", None, "dp"), P("mp", None, None, "dp")),
        check_vma=False,
    )
```

```python
import functools
import jax
import jax.numpy as jnp
from jax import lax
from jax.experimental import pallas as pl
from jax.experimental.pallas import tpu as pltpu
from jax.sharding import PartitionSpec as P

ROWS = 2
BUCKETS = 8
HEAVY = 8
BLK = 128
TOK = 128
ROW_BLOCKS = 40
COL_BLOCKS = 17
CPAD = 18
GRP = 4
GROUPS = TOK // GRP
KIN = GRP * ROW_BLOCKS
KC = GRP * CPAD
SKETCH = ROWS * BUCKETS
OUT_ROWS = HEAVY + SKETCH
DEPTH = GROUPS * KC
TN = (((0,), (0,)), ((), ()))
F32 = jnp.float32
BF16 = jnp.bfloat16
PAIR = 4
BLOCKS = GROUPS // 2
CUTS = 1
SIDE = 8
MODEL = 8


def mate(v, half):
    return (v + 1 if (v + half) % 2 == 0 else v - 1) % SIDE


def near_groups():
    groups = set()
    for m in range(MODEL):
        for y in range(SIDE):
            for z in range(SIDE):
                ys, zs = {y, mate(y, m % 2)}, {z, mate(z, m % 2)}
                groups.add(
                    tuple(
                        (u * SIDE + v) * MODEL + m
                        for u in sorted(ys, key=lambda t: t % 2)
                        for v in sorted(zs, key=lambda t: t % 2)
                    )
                )
    return [list(g) for g in sorted(groups)]


NEAR = near_groups()
FAR = [[(2 * a + i) * SIDE + 2 * b + j for a in range(4) for b in range(4)] for i in range(2) for j in range(2)]


def iota(shape, dim):
    return lax.broadcasted_iota(jnp.int32, shape, dim)


def kernel(
    act_h, cot_h, err_h, bkt_h, sgn_h, heavy_h,
    result,
    act, cot, err4, bkt, sgn, heavy, bkt_s, sgn_s, err, extra, act3, cot3, maps, actb, lhs, hi_a, lo_a, hi_b, lo_b, out, sems, out_sems,
):
    pairs = [
        (bkt_h, bkt), (sgn_h, sgn), (act_h, act), (cot_h, cot),
        (heavy_h, heavy), (bkt_h, bkt_s), (sgn_h, sgn_s), (err_h, err4),
    ]
    copies = [pltpu.make_async_copy(a, b, sems.at[i]) for i, (a, b) in enumerate(pairs)]
    for copy in copies:
        copy.start()
    spread_rows = (iota((KC, COL_BLOCKS), 0) % CPAD == iota((KC, COL_BLOCKS), 1)).astype(F32)
    spread_cols = (iota((ROW_BLOCKS, KIN), 1) % ROW_BLOCKS == iota((ROW_BLOCKS, KIN), 0)).astype(F32)
    own = (iota((KC, KIN), 0) // CPAD == iota((KC, KIN), 1) // ROW_BLOCKS) & (
        iota((KC, KIN), 0) % CPAD < COL_BLOCKS
    )
    copies[0].wait()
    copies[1].wait()
    copies[4].wait()
    times = jnp.ones((COL_BLOCKS, ROW_BLOCKS), F32)
    for k in range(HEAVY):
        a, c = lax.div(heavy[k], COL_BLOCKS), lax.rem(heavy[k], COL_BLOCKS)
        here = (iota(times.shape, 0) == c) & (iota(times.shape, 1) == a)
        times = times - here.astype(F32)

    def spread(x):
        return jnp.dot(jnp.dot(spread_rows, x, preferred_element_type=F32), spread_cols, preferred_element_type=F32)

    for r in range(ROWS):
        weight = spread((2 * sgn[:, r, :] - 1).astype(F32) * times)
        bucket = jnp.where(own, spread(bkt[:, r, :].astype(F32)), -1.0)
        for b in range(0, BUCKETS, 2):
            two = [jnp.where(bucket == bb, weight, 0.0) for bb in (b, b + 1)]
            at = (r * BUCKETS + b) * KC
            maps[at : at + 2 * KC, :] = jnp.concatenate(two, axis=0).astype(BF16)

    copies[2].wait()
    for a in range(ROW_BLOCKS):
        act3[pl.ds(a, TOK, stride=ROW_BLOCKS), :] = act[:, a * BLK : (a + 1) * BLK].astype(F32)
    copies[3].wait()
    for c in range(COL_BLOCKS):
        cot3[pl.ds(c, TOK, stride=CPAD), :] = cot[:, c * BLK : (c + 1) * BLK].astype(F32)
    cot3[pl.ds(COL_BLOCKS, TOK, stride=CPAD), :] = jnp.zeros((TOK, BLK), F32)

    inverse = 1.0 / TOK
    for copy in copies[5:]:
        copy.wait()
    for r in range(ROWS):
        for j in range(2):
            err[j * SKETCH + r * BUCKETS : j * SKETCH + (r + 1) * BUCKETS, :] = err4[0, r, :, j * BLK : (j + 1) * BLK]
    for k in range(HEAVY):
        a = lax.div(heavy[k], COL_BLOCKS)
        c = lax.rem(heavy[k], COL_BLOCKS)
        block = lax.dot_general(
            act3[pl.ds(a, TOK, stride=ROW_BLOCKS), :].astype(BF16),
            cot[:, pl.ds(pl.multiple_of(c * BLK, BLK), BLK)],
            TN,
            preferred_element_type=F32,
        ) * inverse
        out[pl.ds(k, BLK, stride=OUT_ROWS), :] = block

    for j in range(2):
        old = err[j * SKETCH : (j + 1) * SKETCH, :]
        guesses = jnp.zeros((HEAVY, BLK), F32)
        for k in range(HEAVY):
            a, c = lax.div(heavy[k], COL_BLOCKS), lax.rem(heavy[k], COL_BLOCKS)
            signs = [(2 * sgn_s[c, r, a] - 1).astype(F32) for r in range(ROWS)]
            rows = [r * BUCKETS + bkt_s[c, r, a] for r in range(ROWS)]
            guess = jnp.zeros((1, BLK), F32)
            for r in range(ROWS):
                guess = guess + signs[r] * err[pl.ds(j * SKETCH + rows[r], 1), :]
            guess = guess * (1.0 / ROWS)
            guesses = jnp.where(iota((HEAVY, BLK), 0) == k, guess, guesses)
            for r in range(ROWS):
                old = old - jnp.where(iota((SKETCH, BLK), 0) == rows[r], signs[r] * guess, 0.0)
        extra[j, :HEAVY, :] = guesses
        extra[j, HEAVY:, :] = old

    for i in range(BLOCKS):
        for h in range(2):
            actb[i, :, h * BLK : (h + 1) * BLK] = act3[(2 * i + h) * KIN : (2 * i + h + 1) * KIN, :].astype(BF16)
    lhs[...] = cot3[...].T.astype(BF16)

    def weigh(g, i, hi, lo):
        many = jnp.dot(maps[g * PAIR * KC : (g + 1) * PAIR * KC, :], actb[i], preferred_element_type=F32)
        rows = slice(i * 2 * KC, (i + 1) * 2 * KC)
        for j in range(PAIR):
            w = many[j * KC : (j + 1) * KC]
            w = jnp.concatenate([w[:, :BLK], w[:, BLK:]], axis=0)
            top = w.astype(BF16)
            hi[rows, j * BLK : (j + 1) * BLK] = top
            lo[rows, j * BLK : (j + 1) * BLK] = (w - top.astype(F32)).astype(BF16)

    def fold(g, hi, lo):
        for t in range(PAIR // 2):
            total = None
            for part in (hi, lo):
                for k in range(CUTS):
                    deep = slice(k * DEPTH // CUTS, (k + 1) * DEPTH // CUTS)
                    term = jnp.dot(
                        lhs[:, deep], part[deep, 2 * t * BLK : 2 * (t + 1) * BLK], preferred_element_type=F32
                    )
                    total = term if total is None else total + term
                    yield
            for j in range(2):
                at = HEAVY + g * PAIR + 2 * t + j
                out[pl.ds(at, BLK, stride=OUT_ROWS), :] = total[:, j * BLK : (j + 1) * BLK].T * inverse

    steps = SKETCH // PAIR
    slots = [(hi_a, lo_a), (hi_b, lo_b)]
    for i in range(BLOCKS):
        weigh(0, i, *slots[0])
    for g in range(steps):
        sums = fold(g, *slots[g % 2])
        count = PAIR * CUTS
        done = 0
        for i in range(BLOCKS):
            if g + 1 < steps:
                weigh(g + 1, i, *slots[(g + 1) % 2])
            while done * BLOCKS < (i + 1) * count:
                next(sums, None)
                done += 1
        for _ in sums:
            pass

    mine = lax.axis_index("dp") * (2 * OUT_ROWS)
    for j in range(2):
        at = pl.ds(mine + j * OUT_ROWS, OUT_ROWS)
        out[at, :] = out[at, :] + extra[j]

    whole = out.reshape(SIDE // 2, 2, SIDE // 2, 2, 2 * OUT_ROWS, BLK)
    sends = [
        pltpu.make_async_copy(whole.at[:, i, :, j], result.at[2 * i + j], out_sems.at[2 * i + j])
        for i in range(2)
        for j in range(2)
    ]
    for send in sends:
        send.start()
    for send in sends:
        send.wait()


def local_part(activations, cotangent, error_sketch, buckets, sign_bits, heavy_blocks):
    bkt, sgn = buckets.transpose(2, 0, 1), sign_bits.transpose(2, 0, 1)
    hbm = pl.BlockSpec(memory_space=pltpu.HBM)
    return pl.pallas_call(
        kernel,
        out_shape=jax.ShapeDtypeStruct((4, SIDE // 2, SIDE // 2, 2 * OUT_ROWS, BLK), F32),
        in_specs=[hbm] * 6,
        out_specs=hbm,
        scratch_shapes=[
            pltpu.VMEM(activations.shape, BF16),
            pltpu.VMEM(cotangent.shape, BF16),
            pltpu.VMEM(error_sketch.shape, F32),
            pltpu.VMEM(bkt.shape, jnp.int32),
            pltpu.VMEM(sgn.shape, jnp.int32),
            pltpu.SMEM(heavy_blocks.shape, jnp.int32),
            pltpu.SMEM(bkt.shape, jnp.int32),
            pltpu.SMEM(sgn.shape, jnp.int32),
            pltpu.VMEM((2 * SKETCH, BLK), F32),
            pltpu.VMEM((2, OUT_ROWS, BLK), F32),
            pltpu.VMEM((TOK * ROW_BLOCKS, BLK), F32),
            pltpu.VMEM((DEPTH, BLK), F32),
            pltpu.VMEM((SKETCH * KC, KIN), BF16),
            pltpu.VMEM((BLOCKS, KIN, 2 * BLK), BF16),
            pltpu.VMEM((BLK, DEPTH), BF16),
            pltpu.VMEM((DEPTH, PAIR * BLK), BF16),
            pltpu.VMEM((DEPTH, PAIR * BLK), BF16),
            pltpu.VMEM((DEPTH, PAIR * BLK), BF16),
            pltpu.VMEM((DEPTH, PAIR * BLK), BF16),
            pltpu.VMEM((BLK * OUT_ROWS, BLK), F32),
            pltpu.SemaphoreType.DMA((8,)),
            pltpu.SemaphoreType.DMA((4,)),
        ],
        compiler_params=pltpu.CompilerParams(vmem_limit_bytes=60 * 1024 * 1024),
        name="sketch_block",
    )(activations, cotangent, error_sketch, bkt, sgn, heavy_blocks)


def finish(parts, update, new_error):
    total = jnp.sum(parts[...], axis=0)
    for j in range(2):
        cols = slice(j * BLK, (j + 1) * BLK)
        row = j * OUT_ROWS
        update[0, :, cols] = total[row : row + HEAVY]
        for r in range(ROWS):
            first = row + HEAVY + r * BUCKETS
            new_error[0, r, :, cols] = total[first : first + BUCKETS]


def outputs(parts):
    vmem = pl.BlockSpec(memory_space=pltpu.VMEM)
    return pl.pallas_call(
        finish,
        out_shape=(
            jax.ShapeDtypeStruct((1, HEAVY, 2 * BLK), F32),
            jax.ShapeDtypeStruct((1, ROWS, BUCKETS, 2 * BLK), F32),
        ),
        in_specs=[vmem],
        out_specs=(vmem, vmem),
        compiler_params=pltpu.CompilerParams(vmem_limit_bytes=2 * 1024 * 1024),
        name="outputs",
    )(parts)


def body(activations, cotangent, error_sketch, buckets, sign_bits, heavy_blocks):
    local = local_part(activations, cotangent, error_sketch, buckets, sign_bits, heavy_blocks)
    part = lax.all_to_all(local.reshape(4, 32 * OUT_ROWS, BLK), ("dp", "mp"), 0, 0, axis_index_groups=NEAR).sum(axis=0)
    parts = lax.all_to_all(part.reshape(16, 2 * OUT_ROWS, BLK), "dp", 0, 0, axis_index_groups=FAR)
    return outputs(parts)


def solution(mesh):
    return jax.shard_map(
        body,
        mesh=mesh,
        in_specs=(
            P("dp", None),
            P("dp", "mp"),
            P("mp", None, None, "dp"),
            P(None, None, "mp"),
            P(None, None, "mp"),
            P("mp"),
        ),
        out_specs=(P("mp", None, "dp"), P("mp", None, None, "dp")),
        check_vma=False,
    )
```

```python
import functools
import jax
import jax.numpy as jnp
from jax import lax
from jax.experimental import pallas as pl
from jax.experimental.pallas import tpu as pltpu
from jax.sharding import PartitionSpec as P

ROWS = 2
BUCKETS = 8
HEAVY = 8
BLK = 128
TOK = 128
ROW_BLOCKS = 40
COL_BLOCKS = 17
CPAD = 18
GRP = 4
GROUPS = TOK // GRP
KIN = GRP * ROW_BLOCKS
KC = GRP * CPAD
SKETCH = ROWS * BUCKETS
OUT_ROWS = HEAVY + SKETCH
DEPTH = GROUPS * KC
TN = (((0,), (0,)), ((), ()))
F32 = jnp.float32
BF16 = jnp.bfloat16
PAIR = 4
BLOCKS = GROUPS // 2
PARTS = 4
SHARE = TOK // PARTS
CUTS = 1
SIDE = 8
MODEL = 8


def mate(v, half):
    return (v + 1 if (v + half) % 2 == 0 else v - 1) % SIDE


def near_groups():
    groups = set()
    for m in range(MODEL):
        for y in range(SIDE):
            for z in range(SIDE):
                ys, zs = {y, mate(y, m % 2)}, {z, mate(z, m % 2)}
                groups.add(
                    tuple(
                        (u * SIDE + v) * MODEL + m
                        for u in sorted(ys, key=lambda t: t % 2)
                        for v in sorted(zs, key=lambda t: t % 2)
                    )
                )
    return [list(g) for g in sorted(groups)]


NEAR = near_groups()
FAR = [[(2 * a + i) * SIDE + 2 * b + j for a in range(4) for b in range(4)] for i in range(2) for j in range(2)]


def iota(shape, dim):
    return lax.broadcasted_iota(jnp.int32, shape, dim)


def kernel(
    act_h, cot_h, err_h, bkt_h, sgn_h, heavy_h,
    result,
    act, cot, err4, bkt, sgn, heavy, bkt_s, sgn_s, err, extra, act3, cot3, maps, actb, lhs, hi_a, lo_a, hi_b, lo_b, out, sems, out_sems,
):
    pairs = [
        (bkt_h, bkt), (sgn_h, sgn), (act_h.at[:SHARE], act.at[:SHARE]), (cot_h, cot),
        (heavy_h, heavy), (bkt_h, bkt_s), (sgn_h, sgn_s), (err_h, err4),
    ]
    pairs += [(act_h.at[i * SHARE : (i + 1) * SHARE], act.at[i * SHARE : (i + 1) * SHARE]) for i in range(1, PARTS)]
    copies = [pltpu.make_async_copy(a, b, sems.at[i]) for i, (a, b) in enumerate(pairs)]
    for copy in copies:
        copy.start()
    spread_rows = (iota((KC, COL_BLOCKS), 0) % CPAD == iota((KC, COL_BLOCKS), 1)).astype(F32)
    spread_cols = (iota((ROW_BLOCKS, KIN), 1) % ROW_BLOCKS == iota((ROW_BLOCKS, KIN), 0)).astype(F32)
    own = (iota((KC, KIN), 0) // CPAD == iota((KC, KIN), 1) // ROW_BLOCKS) & (
        iota((KC, KIN), 0) % CPAD < COL_BLOCKS
    )
    copies[0].wait()
    copies[1].wait()
    copies[4].wait()
    times = jnp.ones((COL_BLOCKS, ROW_BLOCKS), F32)
    for k in range(HEAVY):
        a, c = lax.div(heavy[k], COL_BLOCKS), lax.rem(heavy[k], COL_BLOCKS)
        here = (iota(times.shape, 0) == c) & (iota(times.shape, 1) == a)
        times = times - here.astype(F32)

    def spread(x):
        return jnp.dot(jnp.dot(spread_rows, x, preferred_element_type=F32), spread_cols, preferred_element_type=F32)

    for r in range(ROWS):
        weight = spread((2 * sgn[:, r, :] - 1).astype(F32) * times)
        bucket = jnp.where(own, spread(bkt[:, r, :].astype(F32)), -1.0)
        for b in range(0, BUCKETS, 2):
            two = [jnp.where(bucket == bb, weight, 0.0) for bb in (b, b + 1)]
            at = (r * BUCKETS + b) * KC
            maps[at : at + 2 * KC, :] = jnp.concatenate(two, axis=0).astype(BF16)

    def lay(part):
        for a in range(ROW_BLOCKS):
            act3[pl.ds(part * SHARE * ROW_BLOCKS + a, SHARE, stride=ROW_BLOCKS), :] = act[
                part * SHARE : (part + 1) * SHARE, a * BLK : (a + 1) * BLK
            ].astype(F32)
        for i in range(part * BLOCKS // PARTS, (part + 1) * BLOCKS // PARTS):
            for h in range(2):
                actb[i, :, h * BLK : (h + 1) * BLK] = act3[(2 * i + h) * KIN : (2 * i + h + 1) * KIN, :].astype(BF16)

    for i in range(PARTS):
        copies[7 + i if i else 2].wait()
        lay(i)
    copies[3].wait()
    for c in range(COL_BLOCKS):
        cot3[pl.ds(c, TOK, stride=CPAD), :] = cot[:, c * BLK : (c + 1) * BLK].astype(F32)
    cot3[pl.ds(COL_BLOCKS, TOK, stride=CPAD), :] = jnp.zeros((TOK, BLK), F32)

    inverse = 1.0 / TOK
    for copy in copies[5:8]:
        copy.wait()
    for r in range(ROWS):
        for j in range(2):
            err[j * SKETCH + r * BUCKETS : j * SKETCH + (r + 1) * BUCKETS, :] = err4[0, r, :, j * BLK : (j + 1) * BLK]
    for k in range(HEAVY):
        a = lax.div(heavy[k], COL_BLOCKS)
        c = lax.rem(heavy[k], COL_BLOCKS)
        block = lax.dot_general(
            act3[pl.ds(a, TOK, stride=ROW_BLOCKS), :].astype(BF16),
            cot[:, pl.ds(pl.multiple_of(c * BLK, BLK), BLK)],
            TN,
            preferred_element_type=F32,
        ) * inverse
        out[pl.ds(k, BLK, stride=OUT_ROWS), :] = block

    for j in range(2):
        old = err[j * SKETCH : (j + 1) * SKETCH, :]
        guesses = jnp.zeros((HEAVY, BLK), F32)
        for k in range(HEAVY):
            a, c = lax.div(heavy[k], COL_BLOCKS), lax.rem(heavy[k], COL_BLOCKS)
            signs = [(2 * sgn_s[c, r, a] - 1).astype(F32) for r in range(ROWS)]
            rows = [r * BUCKETS + bkt_s[c, r, a] for r in range(ROWS)]
            guess = jnp.zeros((1, BLK), F32)
            for r in range(ROWS):
                guess = guess + signs[r] * err[pl.ds(j * SKETCH + rows[r], 1), :]
            guess = guess * (1.0 / ROWS)
            guesses = jnp.where(iota((HEAVY, BLK), 0) == k, guess, guesses)
            for r in range(ROWS):
                old = old - jnp.where(iota((SKETCH, BLK), 0) == rows[r], signs[r] * guess, 0.0)
        extra[j, :HEAVY, :] = guesses
        extra[j, HEAVY:, :] = old

    lhs[...] = cot3[...].T.astype(BF16)

    def weigh(g, i, hi, lo):
        many = jnp.dot(maps[g * PAIR * KC : (g + 1) * PAIR * KC, :], actb[i], preferred_element_type=F32)
        rows = slice(i * 2 * KC, (i + 1) * 2 * KC)
        for j in range(PAIR):
            w = many[j * KC : (j + 1) * KC]
            w = jnp.concatenate([w[:, :BLK], w[:, BLK:]], axis=0)
            top = w.astype(BF16)
            hi[rows, j * BLK : (j + 1) * BLK] = top
            lo[rows, j * BLK : (j + 1) * BLK] = (w - top.astype(F32)).astype(BF16)

    def fold(g, hi, lo):
        for t in range(PAIR // 2):
            total = None
            for part in (hi, lo):
                for k in range(CUTS):
                    deep = slice(k * DEPTH // CUTS, (k + 1) * DEPTH // CUTS)
                    term = jnp.dot(
                        lhs[:, deep], part[deep, 2 * t * BLK : 2 * (t + 1) * BLK], preferred_element_type=F32
                    )
                    total = term if total is None else total + term
                    yield
            for j in range(2):
                at = HEAVY + g * PAIR + 2 * t + j
                out[pl.ds(at, BLK, stride=OUT_ROWS), :] = total[:, j * BLK : (j + 1) * BLK].T * inverse

    mine = lax.axis_index("dp") * (2 * OUT_ROWS)
    whole = out.reshape(SIDE // 2, 2, SIDE // 2, 2, 2, OUT_ROWS, BLK)
    sends = []

    def send(first, count):
        for j in range(2):
            at = pl.ds(mine + j * OUT_ROWS + first, count)
            out[at, :] = out[at, :] + extra[j, first : first + count, :]
        for i in range(2):
            for j in range(2):
                rows = pl.ds(first, count)
                copy = pltpu.make_async_copy(
                    whole.at[:, i, :, j, :, rows], result.at[2 * i + j, :, :, :, rows], out_sems.at[len(sends)]
                )
                copy.start()
                sends.append(copy)

    steps = SKETCH // PAIR
    slots = [(hi_a, lo_a), (hi_b, lo_b)]
    for i in range(BLOCKS):
        weigh(0, i, *slots[0])
    for g in range(steps):
        sums = fold(g, *slots[g % 2])
        count = PAIR * CUTS
        done = 0
        for i in range(BLOCKS):
            if g + 1 < steps:
                weigh(g + 1, i, *slots[(g + 1) % 2])
            while done * BLOCKS < (i + 1) * count:
                next(sums, None)
                done += 1
        for _ in sums:
            pass
        if g == 1:
            send(0, HEAVY + BUCKETS)
    send(HEAVY + BUCKETS, BUCKETS)
    for copy in sends:
        copy.wait()


def local_part(activations, cotangent, error_sketch, buckets, sign_bits, heavy_blocks):
    bkt, sgn = buckets.transpose(2, 0, 1), sign_bits.transpose(2, 0, 1)
    hbm = pl.BlockSpec(memory_space=pltpu.HBM)
    return pl.pallas_call(
        kernel,
        out_shape=jax.ShapeDtypeStruct((4, SIDE // 2, SIDE // 2, 2, OUT_ROWS, BLK), F32),
        in_specs=[hbm] * 6,
        out_specs=hbm,
        scratch_shapes=[
            pltpu.VMEM(activations.shape, BF16),
            pltpu.VMEM(cotangent.shape, BF16),
            pltpu.VMEM(error_sketch.shape, F32),
            pltpu.VMEM(bkt.shape, jnp.int32),
            pltpu.VMEM(sgn.shape, jnp.int32),
            pltpu.SMEM(heavy_blocks.shape, jnp.int32),
            pltpu.SMEM(bkt.shape, jnp.int32),
            pltpu.SMEM(sgn.shape, jnp.int32),
            pltpu.VMEM((2 * SKETCH, BLK), F32),
            pltpu.VMEM((2, OUT_ROWS, BLK), F32),
            pltpu.VMEM((TOK * ROW_BLOCKS, BLK), F32),
            pltpu.VMEM((DEPTH, BLK), F32),
            pltpu.VMEM((SKETCH * KC, KIN), BF16),
            pltpu.VMEM((BLOCKS, KIN, 2 * BLK), BF16),
            pltpu.VMEM((BLK, DEPTH), BF16),
            pltpu.VMEM((DEPTH, PAIR * BLK), BF16),
            pltpu.VMEM((DEPTH, PAIR * BLK), BF16),
            pltpu.VMEM((DEPTH, PAIR * BLK), BF16),
            pltpu.VMEM((DEPTH, PAIR * BLK), BF16),
            pltpu.VMEM((BLK * OUT_ROWS, BLK), F32),
            pltpu.SemaphoreType.DMA((7 + PARTS,)),
            pltpu.SemaphoreType.DMA((8,)),
        ],
        compiler_params=pltpu.CompilerParams(vmem_limit_bytes=60 * 1024 * 1024),
        name="sketch_block",
    )(activations, cotangent, error_sketch, bkt, sgn, heavy_blocks)


def finish(parts, update, new_error):
    total = jnp.sum(parts[...], axis=0)
    for j in range(2):
        cols = slice(j * BLK, (j + 1) * BLK)
        row = j * OUT_ROWS
        update[0, :, cols] = total[row : row + HEAVY]
        for r in range(ROWS):
            first = row + HEAVY + r * BUCKETS
            new_error[0, r, :, cols] = total[first : first + BUCKETS]


def outputs(parts):
    vmem = pl.BlockSpec(memory_space=pltpu.VMEM)
    return pl.pallas_call(
        finish,
        out_shape=(
            jax.ShapeDtypeStruct((1, HEAVY, 2 * BLK), F32),
            jax.ShapeDtypeStruct((1, ROWS, BUCKETS, 2 * BLK), F32),
        ),
        in_specs=[vmem],
        out_specs=(vmem, vmem),
        compiler_params=pltpu.CompilerParams(vmem_limit_bytes=2 * 1024 * 1024),
        name="outputs",
    )(parts)


def body(activations, cotangent, error_sketch, buckets, sign_bits, heavy_blocks):
    local = local_part(activations, cotangent, error_sketch, buckets, sign_bits, heavy_blocks)
    part = lax.all_to_all(local.reshape(4, 32 * OUT_ROWS, BLK), ("dp", "mp"), 0, 0, axis_index_groups=NEAR).sum(axis=0)
    parts = lax.all_to_all(part.reshape(16, 2 * OUT_ROWS, BLK), "dp", 0, 0, axis_index_groups=FAR)
    return outputs(parts)


def solution(mesh):
    return jax.shard_map(
        body,
        mesh=mesh,
        in_specs=(
            P("dp", None),
            P("dp", "mp"),
            P("mp", None, None, "dp"),
            P(None, None, "mp"),
            P(None, None, "mp"),
            P("mp"),
        ),
        out_specs=(P("mp", None, "dp"), P("mp", None, None, "dp")),
        check_vma=False,
    )
```

```python
import functools
import jax
import jax.numpy as jnp
from jax import lax
from jax.experimental import pallas as pl
from jax.experimental.pallas import tpu as pltpu
from jax.sharding import PartitionSpec as P

ROWS = 2
BUCKETS = 8
HEAVY = 8
BLK = 128
TOK = 128
ROW_BLOCKS = 40
COL_BLOCKS = 17
CPAD = 18
GRP = 4
GROUPS = TOK // GRP
KIN = GRP * ROW_BLOCKS
KC = GRP * CPAD
SKETCH = ROWS * BUCKETS
OUT_ROWS = HEAVY + SKETCH
DEPTH = GROUPS * KC
TN = (((0,), (0,)), ((), ()))
F32 = jnp.float32
BF16 = jnp.bfloat16
PAIR = 4
BLOCKS = GROUPS // 2
PARTS = 4
SHARE = TOK // PARTS
CUTS = 1
SIDE = 8
MODEL = 8


def mate(v, half):
    return (v + 1 if (v + half) % 2 == 0 else v - 1) % SIDE


def near_groups():
    groups = set()
    for m in range(MODEL):
        for y in range(SIDE):
            for z in range(SIDE):
                ys, zs = {y, mate(y, m % 2)}, {z, mate(z, m % 2)}
                groups.add(
                    tuple(
                        (u * SIDE + v) * MODEL + m
                        for u in sorted(ys, key=lambda t: t % 2)
                        for v in sorted(zs, key=lambda t: t % 2)
                    )
                )
    return [list(g) for g in sorted(groups)]


NEAR = near_groups()
FAR = [[(2 * a + i) * SIDE + 2 * b + j for a in range(4) for b in range(4)] for i in range(2) for j in range(2)]


def iota(shape, dim):
    return lax.broadcasted_iota(jnp.int32, shape, dim)


def kernel(
    act_h, cot_h, err_h, bkt_h, sgn_h, heavy_h,
    result,
    act, cot, err4, bkt, sgn, heavy, bkt_s, sgn_s, err, extra, act3, cot3, maps, actb, lhs, hi_a, lo_a, hi_b, lo_b, out, sems, out_sems,
):
    pairs = [
        (bkt_h, bkt), (sgn_h, sgn), (act_h.at[:SHARE], act.at[:SHARE]), (cot_h, cot),
        (heavy_h, heavy), (bkt_h, bkt_s), (sgn_h, sgn_s), (err_h, err4),
    ]
    pairs += [(act_h.at[i * SHARE : (i + 1) * SHARE], act.at[i * SHARE : (i + 1) * SHARE]) for i in range(1, PARTS)]
    copies = [pltpu.make_async_copy(a, b, sems.at[i]) for i, (a, b) in enumerate(pairs)]
    for copy in copies:
        copy.start()
    spread_rows = (iota((KC, COL_BLOCKS), 0) % CPAD == iota((KC, COL_BLOCKS), 1)).astype(F32)
    spread_cols = (iota((ROW_BLOCKS, KIN), 1) % ROW_BLOCKS == iota((ROW_BLOCKS, KIN), 0)).astype(F32)
    own = (iota((KC, KIN), 0) // CPAD == iota((KC, KIN), 1) // ROW_BLOCKS) & (
        iota((KC, KIN), 0) % CPAD < COL_BLOCKS
    )
    copies[0].wait()
    copies[1].wait()
    copies[4].wait()
    times = jnp.ones((COL_BLOCKS, ROW_BLOCKS), F32)
    for k in range(HEAVY):
        a, c = lax.div(heavy[k], COL_BLOCKS), lax.rem(heavy[k], COL_BLOCKS)
        here = (iota(times.shape, 0) == c) & (iota(times.shape, 1) == a)
        times = times - here.astype(F32)

    def spread(x):
        return jnp.dot(jnp.dot(spread_rows, x, preferred_element_type=F32), spread_cols, preferred_element_type=F32)

    for r in range(ROWS):
        weight = spread((2 * sgn[:, r, :] - 1).astype(F32) * times)
        bucket = jnp.where(own, spread(bkt[:, r, :].astype(F32)), -1.0)
        for b in range(0, BUCKETS, 2):
            two = [jnp.where(bucket == bb, weight, 0.0) for bb in (b, b + 1)]
            at = (r * BUCKETS + b) * KC
            maps[at : at + 2 * KC, :] = jnp.concatenate(two, axis=0).astype(BF16)

    def lay(part):
        for a in range(ROW_BLOCKS):
            act3[pl.ds(part * SHARE * ROW_BLOCKS + a, SHARE, stride=ROW_BLOCKS), :] = act[
                part * SHARE : (part + 1) * SHARE, a * BLK : (a + 1) * BLK
            ].astype(F32)
        for i in range(part * BLOCKS // PARTS, (part + 1) * BLOCKS // PARTS):
            for h in range(2):
                actb[i, :, h * BLK : (h + 1) * BLK] = act3[(2 * i + h) * KIN : (2 * i + h + 1) * KIN, :].astype(BF16)

    for i in range(PARTS):
        copies[7 + i if i else 2].wait()
        lay(i)
    copies[3].wait()
    for c in range(COL_BLOCKS):
        cot3[pl.ds(c, TOK, stride=CPAD), :] = cot[:, c * BLK : (c + 1) * BLK].astype(F32)
    cot3[pl.ds(COL_BLOCKS, TOK, stride=CPAD), :] = jnp.zeros((TOK, BLK), F32)

    inverse = 1.0 / TOK
    for copy in copies[5:8]:
        copy.wait()
    for r in range(ROWS):
        for j in range(2):
            err[j * SKETCH + r * BUCKETS : j * SKETCH + (r + 1) * BUCKETS, :] = err4[0, r, :, j * BLK : (j + 1) * BLK]
    for k in range(HEAVY):
        a = lax.div(heavy[k], COL_BLOCKS)
        c = lax.rem(heavy[k], COL_BLOCKS)
        block = lax.dot_general(
            act3[pl.ds(a, TOK, stride=ROW_BLOCKS), :].astype(BF16),
            cot[:, pl.ds(pl.multiple_of(c * BLK, BLK), BLK)],
            TN,
            preferred_element_type=F32,
        ) * inverse
        out[pl.ds(k, BLK, stride=OUT_ROWS), :] = block

    for j in range(2):
        old = err[j * SKETCH : (j + 1) * SKETCH, :]
        guesses = jnp.zeros((HEAVY, BLK), F32)
        for k in range(HEAVY):
            a, c = lax.div(heavy[k], COL_BLOCKS), lax.rem(heavy[k], COL_BLOCKS)
            signs = [(2 * sgn_s[c, r, a] - 1).astype(F32) for r in range(ROWS)]
            rows = [r * BUCKETS + bkt_s[c, r, a] for r in range(ROWS)]
            guess = jnp.zeros((1, BLK), F32)
            for r in range(ROWS):
                guess = guess + signs[r] * err[pl.ds(j * SKETCH + rows[r], 1), :]
            guess = guess * (1.0 / ROWS)
            guesses = jnp.where(iota((HEAVY, BLK), 0) == k, guess, guesses)
            for r in range(ROWS):
                old = old - jnp.where(iota((SKETCH, BLK), 0) == rows[r], signs[r] * guess, 0.0)
        extra[j, :HEAVY, :] = guesses
        extra[j, HEAVY:, :] = old

    lhs[...] = cot3[...].T.astype(BF16)

    def weigh(g, i, hi, lo):
        many = jnp.dot(maps[g * PAIR * KC : (g + 1) * PAIR * KC, :], actb[i], preferred_element_type=F32)
        rows = slice(i * 2 * KC, (i + 1) * 2 * KC)
        for j in range(PAIR):
            w = many[j * KC : (j + 1) * KC]
            w = jnp.concatenate([w[:, :BLK], w[:, BLK:]], axis=0)
            top = w.astype(BF16)
            hi[rows, j * BLK : (j + 1) * BLK] = top
            lo[rows, j * BLK : (j + 1) * BLK] = (w - top.astype(F32)).astype(BF16)

    def fold(g, hi, lo):
        for t in range(PAIR // 2):
            total = None
            for part in (hi, lo):
                for k in range(CUTS):
                    deep = slice(k * DEPTH // CUTS, (k + 1) * DEPTH // CUTS)
                    term = jnp.dot(
                        lhs[:, deep], part[deep, 2 * t * BLK : 2 * (t + 1) * BLK], preferred_element_type=F32
                    )
                    total = term if total is None else total + term
                    yield
            for j in range(2):
                at = HEAVY + g * PAIR + 2 * t + j
                out[pl.ds(at, BLK, stride=OUT_ROWS), :] = total[:, j * BLK : (j + 1) * BLK].T * inverse

    steps = SKETCH // PAIR
    slots = [(hi_a, lo_a), (hi_b, lo_b)]
    for i in range(BLOCKS):
        weigh(0, i, *slots[0])
    for g in range(steps):
        sums = fold(g, *slots[g % 2])
        count = PAIR * CUTS
        done = 0
        for i in range(BLOCKS):
            if g + 1 < steps:
                weigh(g + 1, i, *slots[(g + 1) % 2])
            while done * BLOCKS < (i + 1) * count:
                next(sums, None)
                done += 1
        for _ in sums:
            pass

    mine = lax.axis_index("dp") * (2 * OUT_ROWS)
    for j in range(2):
        at = pl.ds(mine + j * OUT_ROWS, OUT_ROWS)
        out[at, :] = out[at, :] + extra[j]

    whole = out.reshape(SIDE // 2, 2, SIDE // 2, 2, 2 * OUT_ROWS, BLK)
    sends = [
        pltpu.make_async_copy(whole.at[:, i, :, j], result.at[2 * i + j], out_sems.at[2 * i + j])
        for i in range(2)
        for j in range(2)
    ]
    for send in sends:
        send.start()
    for send in sends:
        send.wait()


def local_part(activations, cotangent, error_sketch, buckets, sign_bits, heavy_blocks):
    bkt, sgn = buckets.transpose(2, 0, 1), sign_bits.transpose(2, 0, 1)
    hbm = pl.BlockSpec(memory_space=pltpu.HBM)
    return pl.pallas_call(
        kernel,
        out_shape=jax.ShapeDtypeStruct((4, SIDE // 2, SIDE // 2, 2 * OUT_ROWS, BLK), F32),
        in_specs=[hbm] * 6,
        out_specs=hbm,
        scratch_shapes=[
            pltpu.VMEM(activations.shape, BF16),
            pltpu.VMEM(cotangent.shape, BF16),
            pltpu.VMEM(error_sketch.shape, F32),
            pltpu.VMEM(bkt.shape, jnp.int32),
            pltpu.VMEM(sgn.shape, jnp.int32),
            pltpu.SMEM(heavy_blocks.shape, jnp.int32),
            pltpu.SMEM(bkt.shape, jnp.int32),
            pltpu.SMEM(sgn.shape, jnp.int32),
            pltpu.VMEM((2 * SKETCH, BLK), F32),
            pltpu.VMEM((2, OUT_ROWS, BLK), F32),
            pltpu.VMEM((TOK * ROW_BLOCKS, BLK), F32),
            pltpu.VMEM((DEPTH, BLK), F32),
            pltpu.VMEM((SKETCH * KC, KIN), BF16),
            pltpu.VMEM((BLOCKS, KIN, 2 * BLK), BF16),
            pltpu.VMEM((BLK, DEPTH), BF16),
            pltpu.VMEM((DEPTH, PAIR * BLK), BF16),
            pltpu.VMEM((DEPTH, PAIR * BLK), BF16),
            pltpu.VMEM((DEPTH, PAIR * BLK), BF16),
            pltpu.VMEM((DEPTH, PAIR * BLK), BF16),
            pltpu.VMEM((BLK * OUT_ROWS, BLK), F32),
            pltpu.SemaphoreType.DMA((7 + PARTS,)),
            pltpu.SemaphoreType.DMA((4,)),
        ],
        compiler_params=pltpu.CompilerParams(vmem_limit_bytes=44 * 1024 * 1024),
        name="sketch_block",
    )(*(pltpu.with_memory_space_constraint(x, pltpu.HBM) for x in (activations, cotangent, error_sketch, bkt, sgn, heavy_blocks)))


def finish(parts, update, new_error):
    total = jnp.sum(parts[...], axis=0)
    for j in range(2):
        cols = slice(j * BLK, (j + 1) * BLK)
        row = j * OUT_ROWS
        update[0, :, cols] = total[row : row + HEAVY]
        for r in range(ROWS):
            first = row + HEAVY + r * BUCKETS
            new_error[0, r, :, cols] = total[first : first + BUCKETS]


def outputs(parts):
    vmem = pl.BlockSpec(memory_space=pltpu.VMEM)
    return pl.pallas_call(
        finish,
        out_shape=(
            jax.ShapeDtypeStruct((1, HEAVY, 2 * BLK), F32),
            jax.ShapeDtypeStruct((1, ROWS, BUCKETS, 2 * BLK), F32),
        ),
        in_specs=[vmem],
        out_specs=(vmem, vmem),
        compiler_params=pltpu.CompilerParams(vmem_limit_bytes=2 * 1024 * 1024),
        name="outputs",
    )(parts)


def body(activations, cotangent, error_sketch, buckets, sign_bits, heavy_blocks):
    local = local_part(activations, cotangent, error_sketch, buckets, sign_bits, heavy_blocks)
    part = lax.all_to_all(local.reshape(4, 32 * OUT_ROWS, BLK), ("dp", "mp"), 0, 0, axis_index_groups=NEAR).sum(axis=0)
    parts = lax.all_to_all(part.reshape(16, 2 * OUT_ROWS, BLK), "dp", 0, 0, axis_index_groups=FAR)
    return outputs(parts)


def solution(mesh):
    return jax.shard_map(
        body,
        mesh=mesh,
        in_specs=(
            P("dp", None),
            P("dp", "mp"),
            P("mp", None, None, "dp"),
            P(None, None, "mp"),
            P(None, None, "mp"),
            P("mp"),
        ),
        out_specs=(P("mp", None, "dp"), P("mp", None, None, "dp")),
        check_vma=False,
    )
```

```python
import functools
import jax
import jax.numpy as jnp
from jax import lax
from jax.experimental import pallas as pl
from jax.experimental.pallas import tpu as pltpu
from jax.sharding import PartitionSpec as P

ROWS = 2
BUCKETS = 8
HEAVY = 8
BLK = 128
TOK = 128
ROW_BLOCKS = 40
COL_BLOCKS = 17
CPAD = 18
GRP = 4
GROUPS = TOK // GRP
KIN = GRP * ROW_BLOCKS
KC = GRP * CPAD
SKETCH = ROWS * BUCKETS
OUT_ROWS = HEAVY + SKETCH
DEPTH = GROUPS * KC
TN = (((0,), (0,)), ((), ()))
F32 = jnp.float32
BF16 = jnp.bfloat16
PAIR = 4
BLOCKS = GROUPS // 2
PARTS = 4
SHARE = TOK // PARTS
CUTS = 1
SIDE = 8
MODEL = 8


def mate(v, half):
    return (v + 1 if (v + half) % 2 == 0 else v - 1) % SIDE


def near_groups():
    groups = set()
    for m in range(MODEL):
        for y in range(SIDE):
            for z in range(SIDE):
                ys, zs = {y, mate(y, 1 - m % 2)}, {z, mate(z, 1 - m % 2)}
                groups.add(
                    tuple(
                        (u * SIDE + v) * MODEL + m
                        for u in sorted(ys, key=lambda t: t % 2)
                        for v in sorted(zs, key=lambda t: t % 2)
                    )
                )
    return [list(g) for g in sorted(groups)]


NEAR = near_groups()
FAR = [[(2 * a + i) * SIDE + 2 * b + j for a in range(4) for b in range(4)] for i in range(2) for j in range(2)]


def iota(shape, dim):
    return lax.broadcasted_iota(jnp.int32, shape, dim)


def kernel(
    act_h, cot_h, err_h, bkt_h, sgn_h, heavy_h,
    result,
    act, cot, err4, bkt, sgn, heavy, bkt_s, sgn_s, err, extra, act3, cot3, maps, actb, lhs, hi_a, lo_a, hi_b, lo_b, out, sems, out_sems,
):
    pairs = [
        (bkt_h, bkt), (sgn_h, sgn), (act_h.at[:SHARE], act.at[:SHARE]), (cot_h, cot),
        (heavy_h, heavy), (bkt_h, bkt_s), (sgn_h, sgn_s), (err_h, err4),
    ]
    pairs += [(act_h.at[i * SHARE : (i + 1) * SHARE], act.at[i * SHARE : (i + 1) * SHARE]) for i in range(1, PARTS)]
    copies = [pltpu.make_async_copy(a, b, sems.at[i]) for i, (a, b) in enumerate(pairs)]
    for copy in copies:
        copy.start()
    spread_rows = (iota((KC, COL_BLOCKS), 0) % CPAD == iota((KC, COL_BLOCKS), 1)).astype(F32)
    spread_cols = (iota((ROW_BLOCKS, KIN), 1) % ROW_BLOCKS == iota((ROW_BLOCKS, KIN), 0)).astype(F32)
    own = (iota((KC, KIN), 0) // CPAD == iota((KC, KIN), 1) // ROW_BLOCKS) & (
        iota((KC, KIN), 0) % CPAD < COL_BLOCKS
    )
    copies[0].wait()
    copies[1].wait()
    copies[4].wait()
    times = jnp.ones((COL_BLOCKS, ROW_BLOCKS), F32)
    for k in range(HEAVY):
        a, c = lax.div(heavy[k], COL_BLOCKS), lax.rem(heavy[k], COL_BLOCKS)
        here = (iota(times.shape, 0) == c) & (iota(times.shape, 1) == a)
        times = times - here.astype(F32)

    def spread(x):
        return jnp.dot(jnp.dot(spread_rows, x, preferred_element_type=F32), spread_cols, preferred_element_type=F32)

    for r in range(ROWS):
        weight = spread((2 * sgn[:, r, :] - 1).astype(F32) * times)
        bucket = jnp.where(own, spread(bkt[:, r, :].astype(F32)), -1.0)
        for b in range(0, BUCKETS, 2):
            two = [jnp.where(bucket == bb, weight, 0.0) for bb in (b, b + 1)]
            at = (r * BUCKETS + b) * KC
            maps[at : at + 2 * KC, :] = jnp.concatenate(two, axis=0).astype(BF16)

    def lay(part):
        for a in range(ROW_BLOCKS):
            act3[pl.ds(part * SHARE * ROW_BLOCKS + a, SHARE, stride=ROW_BLOCKS), :] = act[
                part * SHARE : (part + 1) * SHARE, a * BLK : (a + 1) * BLK
            ].astype(F32)
        for i in range(part * BLOCKS // PARTS, (part + 1) * BLOCKS // PARTS):
            for h in range(2):
                actb[i, :, h * BLK : (h + 1) * BLK] = act3[(2 * i + h) * KIN : (2 * i + h + 1) * KIN, :].astype(BF16)

    for i in range(PARTS):
        copies[7 + i if i else 2].wait()
        lay(i)
    copies[3].wait()
    for c in range(COL_BLOCKS):
        cot3[pl.ds(c, TOK, stride=CPAD), :] = cot[:, c * BLK : (c + 1) * BLK].astype(F32)
    cot3[pl.ds(COL_BLOCKS, TOK, stride=CPAD), :] = jnp.zeros((TOK, BLK), F32)

    inverse = 1.0 / TOK
    for copy in copies[5:8]:
        copy.wait()
    for r in range(ROWS):
        for j in range(2):
            err[j * SKETCH + r * BUCKETS : j * SKETCH + (r + 1) * BUCKETS, :] = err4[0, r, :, j * BLK : (j + 1) * BLK]
    for k in range(HEAVY):
        a = lax.div(heavy[k], COL_BLOCKS)
        c = lax.rem(heavy[k], COL_BLOCKS)
        block = lax.dot_general(
            act3[pl.ds(a, TOK, stride=ROW_BLOCKS), :].astype(BF16),
            cot[:, pl.ds(pl.multiple_of(c * BLK, BLK), BLK)],
            TN,
            preferred_element_type=F32,
        ) * inverse
        out[pl.ds(k, BLK, stride=OUT_ROWS), :] = block

    for j in range(2):
        old = err[j * SKETCH : (j + 1) * SKETCH, :]
        guesses = jnp.zeros((HEAVY, BLK), F32)
        for k in range(HEAVY):
            a, c = lax.div(heavy[k], COL_BLOCKS), lax.rem(heavy[k], COL_BLOCKS)
            signs = [(2 * sgn_s[c, r, a] - 1).astype(F32) for r in range(ROWS)]
            rows = [r * BUCKETS + bkt_s[c, r, a] for r in range(ROWS)]
            guess = jnp.zeros((1, BLK), F32)
            for r in range(ROWS):
                guess = guess + signs[r] * err[pl.ds(j * SKETCH + rows[r], 1), :]
            guess = guess * (1.0 / ROWS)
            guesses = jnp.where(iota((HEAVY, BLK), 0) == k, guess, guesses)
            for r in range(ROWS):
                old = old - jnp.where(iota((SKETCH, BLK), 0) == rows[r], signs[r] * guess, 0.0)
        extra[j, :HEAVY, :] = guesses
        extra[j, HEAVY:, :] = old

    lhs[...] = cot3[...].T.astype(BF16)

    def weigh(g, i, hi, lo):
        many = jnp.dot(maps[g * PAIR * KC : (g + 1) * PAIR * KC, :], actb[i], preferred_element_type=F32)
        rows = slice(i * 2 * KC, (i + 1) * 2 * KC)
        for j in range(PAIR):
            w = many[j * KC : (j + 1) * KC]
            w = jnp.concatenate([w[:, :BLK], w[:, BLK:]], axis=0)
            top = w.astype(BF16)
            hi[rows, j * BLK : (j + 1) * BLK] = top
            lo[rows, j * BLK : (j + 1) * BLK] = (w - top.astype(F32)).astype(BF16)

    def fold(g, hi, lo):
        for t in range(PAIR // 2):
            total = None
            for part in (hi, lo):
                for k in range(CUTS):
                    deep = slice(k * DEPTH // CUTS, (k + 1) * DEPTH // CUTS)
                    term = jnp.dot(
                        lhs[:, deep], part[deep, 2 * t * BLK : 2 * (t + 1) * BLK], preferred_element_type=F32
                    )
                    total = term if total is None else total + term
                    yield
            for j in range(2):
                at = HEAVY + g * PAIR + 2 * t + j
                out[pl.ds(at, BLK, stride=OUT_ROWS), :] = total[:, j * BLK : (j + 1) * BLK].T * inverse

    steps = SKETCH // PAIR
    slots = [(hi_a, lo_a), (hi_b, lo_b)]
    for i in range(BLOCKS):
        weigh(0, i, *slots[0])
    for g in range(steps):
        sums = fold(g, *slots[g % 2])
        count = PAIR * CUTS
        done = 0
        for i in range(BLOCKS):
            if g + 1 < steps:
                weigh(g + 1, i, *slots[(g + 1) % 2])
            while done * BLOCKS < (i + 1) * count:
                next(sums, None)
                done += 1
        for _ in sums:
            pass

    mine = lax.axis_index("dp") * (2 * OUT_ROWS)
    for j in range(2):
        at = pl.ds(mine + j * OUT_ROWS, OUT_ROWS)
        out[at, :] = out[at, :] + extra[j]

    whole = out.reshape(SIDE // 2, 2, SIDE // 2, 2, 2 * OUT_ROWS, BLK)
    sends = [
        pltpu.make_async_copy(whole.at[:, i, :, j], result.at[2 * i + j], out_sems.at[2 * i + j])
        for i in range(2)
        for j in range(2)
    ]
    for send in sends:
        send.start()
    for send in sends:
        send.wait()


def local_part(activations, cotangent, error_sketch, buckets, sign_bits, heavy_blocks):
    bkt, sgn = buckets.transpose(2, 0, 1), sign_bits.transpose(2, 0, 1)
    hbm = pl.BlockSpec(memory_space=pltpu.HBM)
    return pl.pallas_call(
        kernel,
        out_shape=jax.ShapeDtypeStruct((4, SIDE // 2, SIDE // 2, 2 * OUT_ROWS, BLK), F32),
        in_specs=[hbm] * 6,
        out_specs=hbm,
        scratch_shapes=[
            pltpu.VMEM(activations.shape, BF16),
            pltpu.VMEM(cotangent.shape, BF16),
            pltpu.VMEM(error_sketch.shape, F32),
            pltpu.VMEM(bkt.shape, jnp.int32),
            pltpu.VMEM(sgn.shape, jnp.int32),
            pltpu.SMEM(heavy_blocks.shape, jnp.int32),
            pltpu.SMEM(bkt.shape, jnp.int32),
            pltpu.SMEM(sgn.shape, jnp.int32),
            pltpu.VMEM((2 * SKETCH, BLK), F32),
            pltpu.VMEM((2, OUT_ROWS, BLK), F32),
            pltpu.VMEM((TOK * ROW_BLOCKS, BLK), F32),
            pltpu.VMEM((DEPTH, BLK), F32),
            pltpu.VMEM((SKETCH * KC, KIN), BF16),
            pltpu.VMEM((BLOCKS, KIN, 2 * BLK), BF16),
            pltpu.VMEM((BLK, DEPTH), BF16),
            pltpu.VMEM((DEPTH, PAIR * BLK), BF16),
            pltpu.VMEM((DEPTH, PAIR * BLK), BF16),
            pltpu.VMEM((DEPTH, PAIR * BLK), BF16),
            pltpu.VMEM((DEPTH, PAIR * BLK), BF16),
            pltpu.VMEM((BLK * OUT_ROWS, BLK), F32),
            pltpu.SemaphoreType.DMA((7 + PARTS,)),
            pltpu.SemaphoreType.DMA((4,)),
        ],
        compiler_params=pltpu.CompilerParams(vmem_limit_bytes=44 * 1024 * 1024),
        name="sketch_block",
    )(*(pltpu.with_memory_space_constraint(x, pltpu.HBM) for x in (activations, cotangent, error_sketch, bkt, sgn, heavy_blocks)))


def finish(parts, update, new_error):
    total = jnp.sum(parts[...], axis=0)
    for j in range(2):
        cols = slice(j * BLK, (j + 1) * BLK)
        row = j * OUT_ROWS
        update[0, :, cols] = total[row : row + HEAVY]
        for r in range(ROWS):
            first = row + HEAVY + r * BUCKETS
            new_error[0, r, :, cols] = total[first : first + BUCKETS]


def outputs(parts):
    vmem = pl.BlockSpec(memory_space=pltpu.VMEM)
    return pl.pallas_call(
        finish,
        out_shape=(
            jax.ShapeDtypeStruct((1, HEAVY, 2 * BLK), F32),
            jax.ShapeDtypeStruct((1, ROWS, BUCKETS, 2 * BLK), F32),
        ),
        in_specs=[vmem],
        out_specs=(vmem, vmem),
        compiler_params=pltpu.CompilerParams(vmem_limit_bytes=2 * 1024 * 1024),
        name="outputs",
    )(parts)


def body(activations, cotangent, error_sketch, buckets, sign_bits, heavy_blocks):
    local = local_part(activations, cotangent, error_sketch, buckets, sign_bits, heavy_blocks)
    part = lax.all_to_all(local.reshape(4, 32 * OUT_ROWS, BLK), ("dp", "mp"), 0, 0, axis_index_groups=NEAR).sum(axis=0)
    parts = lax.all_to_all(part.reshape(16, 2 * OUT_ROWS, BLK), "dp", 0, 0, axis_index_groups=FAR)
    return outputs(parts)


def solution(mesh):
    return jax.shard_map(
        body,
        mesh=mesh,
        in_specs=(
            P("dp", None),
            P("dp", "mp"),
            P("mp", None, None, "dp"),
            P(None, None, "mp"),
            P(None, None, "mp"),
            P("mp"),
        ),
        out_specs=(P("mp", None, "dp"), P("mp", None, None, "dp")),
        check_vma=False,
    )
```

```python
import functools
import jax
import jax.numpy as jnp
from jax import lax
from jax.experimental import pallas as pl
from jax.experimental.pallas import tpu as pltpu
from jax.sharding import PartitionSpec as P

ROWS = 2
BUCKETS = 8
HEAVY = 8
BLK = 128
TOK = 128
ROW_BLOCKS = 40
COL_BLOCKS = 17
CPAD = 18
GRP = 4
GROUPS = TOK // GRP
KIN = GRP * ROW_BLOCKS
KC = GRP * CPAD
SKETCH = ROWS * BUCKETS
OUT_ROWS = HEAVY + SKETCH
DEPTH = GROUPS * KC
TN = (((0,), (0,)), ((), ()))
F32 = jnp.float32
BF16 = jnp.bfloat16
PAIR = 4
BLOCKS = GROUPS // 2
PARTS = 4
SHARE = TOK // PARTS
CUTS = 1
SIDE = 8
MODEL = 8


def mate(v, half):
    return (v + 1 if (v + half) % 2 == 0 else v - 1) % SIDE


def near_groups():
    groups = set()
    for m in range(MODEL):
        for y in range(SIDE):
            for z in range(SIDE):
                ys, zs = {y, mate(y, 1 - m % 2)}, {z, mate(z, 1 - m % 2)}
                groups.add(
                    tuple(
                        (u * SIDE + v) * MODEL + m
                        for u in sorted(ys, key=lambda t: t % 2)
                        for v in sorted(zs, key=lambda t: t % 2)
                    )
                )
    return [list(g) for g in sorted(groups)]


NEAR = near_groups()
FAR = [[(2 * a + i) * SIDE + 2 * b + j for a in range(4) for b in range(4)] for i in range(2) for j in range(2)]


def iota(shape, dim):
    return lax.broadcasted_iota(jnp.int32, shape, dim)


def kernel(
    act_h, cot_h, err_h, bkt_h, sgn_h, heavy_h,
    out,
    act, cot, err4, bkt, sgn, heavy, bkt_s, sgn_s, err, extra, act3, cot3, maps, actb, lhs, hi_a, lo_a, hi_b, lo_b, sems,
):
    pairs = [
        (bkt_h, bkt), (sgn_h, sgn), (act_h.at[:SHARE], act.at[:SHARE]), (cot_h, cot),
        (heavy_h, heavy), (bkt_h, bkt_s), (sgn_h, sgn_s), (err_h, err4),
    ]
    pairs += [(act_h.at[i * SHARE : (i + 1) * SHARE], act.at[i * SHARE : (i + 1) * SHARE]) for i in range(1, PARTS)]
    copies = [pltpu.make_async_copy(a, b, sems.at[i]) for i, (a, b) in enumerate(pairs)]
    for copy in copies:
        copy.start()
    spread_rows = (iota((KC, COL_BLOCKS), 0) % CPAD == iota((KC, COL_BLOCKS), 1)).astype(F32)
    spread_cols = (iota((ROW_BLOCKS, KIN), 1) % ROW_BLOCKS == iota((ROW_BLOCKS, KIN), 0)).astype(F32)
    own = (iota((KC, KIN), 0) // CPAD == iota((KC, KIN), 1) // ROW_BLOCKS) & (
        iota((KC, KIN), 0) % CPAD < COL_BLOCKS
    )
    copies[0].wait()
    copies[1].wait()
    copies[4].wait()
    times = jnp.ones((COL_BLOCKS, ROW_BLOCKS), F32)
    for k in range(HEAVY):
        a, c = lax.div(heavy[k], COL_BLOCKS), lax.rem(heavy[k], COL_BLOCKS)
        here = (iota(times.shape, 0) == c) & (iota(times.shape, 1) == a)
        times = times - here.astype(F32)

    def spread(x):
        return jnp.dot(jnp.dot(spread_rows, x, preferred_element_type=F32), spread_cols, preferred_element_type=F32)

    for r in range(ROWS):
        weight = spread((2 * sgn[:, r, :] - 1).astype(F32) * times)
        bucket = jnp.where(own, spread(bkt[:, r, :].astype(F32)), -1.0)
        for b in range(0, BUCKETS, 2):
            two = [jnp.where(bucket == bb, weight, 0.0) for bb in (b, b + 1)]
            at = (r * BUCKETS + b) * KC
            maps[at : at + 2 * KC, :] = jnp.concatenate(two, axis=0).astype(BF16)

    def lay(part):
        for a in range(ROW_BLOCKS):
            act3[pl.ds(part * SHARE * ROW_BLOCKS + a, SHARE, stride=ROW_BLOCKS), :] = act[
                part * SHARE : (part + 1) * SHARE, a * BLK : (a + 1) * BLK
            ].astype(F32)
        for i in range(part * BLOCKS // PARTS, (part + 1) * BLOCKS // PARTS):
            for h in range(2):
                actb[i, :, h * BLK : (h + 1) * BLK] = act3[(2 * i + h) * KIN : (2 * i + h + 1) * KIN, :].astype(BF16)

    for i in range(PARTS):
        copies[7 + i if i else 2].wait()
        lay(i)
    copies[3].wait()
    for c in range(COL_BLOCKS):
        cot3[pl.ds(c, TOK, stride=CPAD), :] = cot[:, c * BLK : (c + 1) * BLK].astype(F32)
    cot3[pl.ds(COL_BLOCKS, TOK, stride=CPAD), :] = jnp.zeros((TOK, BLK), F32)

    inverse = 1.0 / TOK
    for copy in copies[5:8]:
        copy.wait()
    for r in range(ROWS):
        for j in range(2):
            err[j * SKETCH + r * BUCKETS : j * SKETCH + (r + 1) * BUCKETS, :] = err4[0, r, :, j * BLK : (j + 1) * BLK]
    for k in range(HEAVY):
        a = lax.div(heavy[k], COL_BLOCKS)
        c = lax.rem(heavy[k], COL_BLOCKS)
        block = lax.dot_general(
            act3[pl.ds(a, TOK, stride=ROW_BLOCKS), :].astype(BF16),
            cot[:, pl.ds(pl.multiple_of(c * BLK, BLK), BLK)],
            TN,
            preferred_element_type=F32,
        ) * inverse
        out[pl.ds(k, BLK, stride=OUT_ROWS), :] = block

    for j in range(2):
        old = err[j * SKETCH : (j + 1) * SKETCH, :]
        guesses = jnp.zeros((HEAVY, BLK), F32)
        for k in range(HEAVY):
            a, c = lax.div(heavy[k], COL_BLOCKS), lax.rem(heavy[k], COL_BLOCKS)
            signs = [(2 * sgn_s[c, r, a] - 1).astype(F32) for r in range(ROWS)]
            rows = [r * BUCKETS + bkt_s[c, r, a] for r in range(ROWS)]
            guess = jnp.zeros((1, BLK), F32)
            for r in range(ROWS):
                guess = guess + signs[r] * err[pl.ds(j * SKETCH + rows[r], 1), :]
            guess = guess * (1.0 / ROWS)
            guesses = jnp.where(iota((HEAVY, BLK), 0) == k, guess, guesses)
            for r in range(ROWS):
                old = old - jnp.where(iota((SKETCH, BLK), 0) == rows[r], signs[r] * guess, 0.0)
        extra[j, :HEAVY, :] = guesses
        extra[j, HEAVY:, :] = old

    lhs[...] = cot3[...].T.astype(BF16)

    def weigh(g, i, hi, lo):
        many = jnp.dot(maps[g * PAIR * KC : (g + 1) * PAIR * KC, :], actb[i], preferred_element_type=F32)
        rows = slice(i * 2 * KC, (i + 1) * 2 * KC)
        for j in range(PAIR):
            w = many[j * KC : (j + 1) * KC]
            w = jnp.concatenate([w[:, :BLK], w[:, BLK:]], axis=0)
            top = w.astype(BF16)
            hi[rows, j * BLK : (j + 1) * BLK] = top
            lo[rows, j * BLK : (j + 1) * BLK] = (w - top.astype(F32)).astype(BF16)

    def fold(g, hi, lo):
        for t in range(PAIR // 2):
            total = None
            for part in (hi, lo):
                for k in range(CUTS):
                    deep = slice(k * DEPTH // CUTS, (k + 1) * DEPTH // CUTS)
                    term = jnp.dot(
                        lhs[:, deep], part[deep, 2 * t * BLK : 2 * (t + 1) * BLK], preferred_element_type=F32
                    )
                    total = term if total is None else total + term
                    yield
            for j in range(2):
                at = HEAVY + g * PAIR + 2 * t + j
                out[pl.ds(at, BLK, stride=OUT_ROWS), :] = total[:, j * BLK : (j + 1) * BLK].T * inverse

    steps = SKETCH // PAIR
    slots = [(hi_a, lo_a), (hi_b, lo_b)]
    for i in range(BLOCKS):
        weigh(0, i, *slots[0])
    for g in range(steps):
        sums = fold(g, *slots[g % 2])
        count = PAIR * CUTS
        done = 0
        for i in range(BLOCKS):
            if g + 1 < steps:
                weigh(g + 1, i, *slots[(g + 1) % 2])
            while done * BLOCKS < (i + 1) * count:
                next(sums, None)
                done += 1
        for _ in sums:
            pass

    mine = lax.axis_index("dp") * (2 * OUT_ROWS)
    for j in range(2):
        at = pl.ds(mine + j * OUT_ROWS, OUT_ROWS)
        out[at, :] = out[at, :] + extra[j]


def local_part(activations, cotangent, error_sketch, buckets, sign_bits, heavy_blocks):
    bkt, sgn = buckets.transpose(2, 0, 1), sign_bits.transpose(2, 0, 1)
    hbm = pl.BlockSpec(memory_space=pltpu.HBM)
    return pl.pallas_call(
        kernel,
        out_shape=jax.ShapeDtypeStruct((BLK * OUT_ROWS, BLK), F32),
        in_specs=[hbm] * 6,
        out_specs=pl.BlockSpec(memory_space=pltpu.VMEM),
        scratch_shapes=[
            pltpu.VMEM(activations.shape, BF16),
            pltpu.VMEM(cotangent.shape, BF16),
            pltpu.VMEM(error_sketch.shape, F32),
            pltpu.VMEM(bkt.shape, jnp.int32),
            pltpu.VMEM(sgn.shape, jnp.int32),
            pltpu.SMEM(heavy_blocks.shape, jnp.int32),
            pltpu.SMEM(bkt.shape, jnp.int32),
            pltpu.SMEM(sgn.shape, jnp.int32),
            pltpu.VMEM((2 * SKETCH, BLK), F32),
            pltpu.VMEM((2, OUT_ROWS, BLK), F32),
            pltpu.VMEM((TOK * ROW_BLOCKS, BLK), F32),
            pltpu.VMEM((DEPTH, BLK), F32),
            pltpu.VMEM((SKETCH * KC, KIN), BF16),
            pltpu.VMEM((BLOCKS, KIN, 2 * BLK), BF16),
            pltpu.VMEM((BLK, DEPTH), BF16),
            pltpu.VMEM((DEPTH, PAIR * BLK), BF16),
            pltpu.VMEM((DEPTH, PAIR * BLK), BF16),
            pltpu.VMEM((DEPTH, PAIR * BLK), BF16),
            pltpu.VMEM((DEPTH, PAIR * BLK), BF16),
            pltpu.SemaphoreType.DMA((7 + PARTS,)),
        ],
        compiler_params=pltpu.CompilerParams(vmem_limit_bytes=44 * 1024 * 1024),
        name="sketch_block",
    )(*(pltpu.with_memory_space_constraint(x, pltpu.HBM) for x in (activations, cotangent, error_sketch, bkt, sgn, heavy_blocks)))


def finish(parts, update, new_error):
    total = jnp.sum(parts[...], axis=0)
    for j in range(2):
        cols = slice(j * BLK, (j + 1) * BLK)
        row = j * OUT_ROWS
        update[0, :, cols] = total[row : row + HEAVY]
        for r in range(ROWS):
            first = row + HEAVY + r * BUCKETS
            new_error[0, r, :, cols] = total[first : first + BUCKETS]


def outputs(parts):
    vmem = pl.BlockSpec(memory_space=pltpu.VMEM)
    return pl.pallas_call(
        finish,
        out_shape=(
            jax.ShapeDtypeStruct((1, HEAVY, 2 * BLK), F32),
            jax.ShapeDtypeStruct((1, ROWS, BUCKETS, 2 * BLK), F32),
        ),
        in_specs=[vmem],
        out_specs=(vmem, vmem),
        compiler_params=pltpu.CompilerParams(vmem_limit_bytes=2 * 1024 * 1024),
        name="outputs",
    )(parts)


def body(activations, cotangent, error_sketch, buckets, sign_bits, heavy_blocks):
    local = local_part(activations, cotangent, error_sketch, buckets, sign_bits, heavy_blocks)
    local = local.reshape(SIDE // 2, 2, SIDE // 2, 2, 2 * OUT_ROWS, BLK).transpose(1, 3, 0, 2, 4, 5)
    part = lax.all_to_all(local.reshape(4, 32 * OUT_ROWS, BLK), ("dp", "mp"), 0, 0, axis_index_groups=NEAR).sum(axis=0)
    parts = lax.all_to_all(part.reshape(16, 2 * OUT_ROWS, BLK), "dp", 0, 0, axis_index_groups=FAR)
    return outputs(parts)


def solution(mesh):
    return jax.shard_map(
        body,
        mesh=mesh,
        in_specs=(
            P("dp", None),
            P("dp", "mp"),
            P("mp", None, None, "dp"),
            P(None, None, "mp"),
            P(None, None, "mp"),
            P("mp"),
        ),
        out_specs=(P("mp", None, "dp"), P("mp", None, None, "dp")),
        check_vma=False,
    )
```
